256 devices in a mesh: tm: 16 (over y, x), panel: 16 (over z, core).
Axes of the slice: x: 4, y: 4, z: 8, core: 2. Of those that a mesh axis runs over, the one named last changes fastest.
Arguments:
- gain: float32 [32, 512, 512], P('tm', 'panel'), may hold values from -0.2 to 1
- cond_cov: float32 [32, 512, 512], P('tm', 'panel'), may hold values from -0.01 to 0.1, as said below
- pred_mean: float32 [32, 512], P('tm', 'panel'), may hold values from -4 to 4
- correction: float32 [32, 512], P('tm', 'panel'), may hold values from -4 to 4
- spread: float32 [512], P('panel'), may hold values from 0.05 to 0.5
- observed: int32 [32, 64], P('tm', 'panel'), may hold values 0 or 1
Outputs:
- smoothed_mean: float32 [32, 512], P('tm', 'panel')
- smoothed_cov: float32 [32, 512, 512], P('tm', 'panel')
The draws below stay inside these ranges and needn't reach their ends.
Inputs may be any that keep to these rules, and one draw needn't show every extreme that they name: Each cond_cov[k] is symmetric.
All inputs are finite; a program needn't handle non-finite values. No bound on the sum of `observed` on one device may be relied on, other than what follows from the above.
Results may differ from the reference program's by a relative error of at most 0.0003.
Values sent between devices are 32-bit elements; how exact they have to be, the bound alone decides.
No kernel may reach another device: no remote copies, remote signals or barrier semaphores. Data moves between devices by JAX's collectives and lax.ppermute only.
A program may use at most 128 MiB of HBM per device.

```python
import math
import jax
import jax.numpy as jnp
from jax import lax

N = 512
BLOCKS = 64
EPOCH_COUNT_ALL = 32


def diagonal_mask():
    row_ids = lax.broadcasted_iota(jnp.int32, (N, N), 0)
    col_ids = lax.broadcasted_iota(jnp.int32, (N, N), 1)
    return (row_ids == col_ids).astype(jnp.float32)


def draw_gain(key, part):
    key = jax.random.fold_in(key, 11)
    key_horizon = jax.random.fold_in(key, 1)
    key_mixing = jax.random.fold_in(key, 2)
    random_seed_pairs = jax.random.fold_in(key, 3)
    random_seed_lengths = jax.random.fold_in(key, 4)
    horizon = jnp.exp(jax.random.uniform(key_horizon, (N,), jnp.float32, math.log(30.0), math.log(4.0 * EPOCH_COUNT_ALL)))
    mixing = jax.random.truncated_normal(key_mixing, -4.0, 4.0, (EPOCH_COUNT_ALL, N, N), jnp.float32)
    persistence_weight = 0.985 * jnp.exp(-1.0 / horizon)
    absent_reading_spans = jnp.where(jax.random.uniform(random_seed_pairs, (EPOCH_COUNT_ALL,), jnp.float32) < 2.0 / EPOCH_COUNT_ALL, jax.random.uniform(random_seed_lengths, (EPOCH_COUNT_ALL,), jnp.float32, 0.5, 0.8), 1.0)
    diagonal_on = diagonal_mask()
    scaled = mixing * (0.2 / math.sqrt(N))
    reading_numbers = persistence_weight[None, :] * absent_reading_spans[:, None]
    return scaled * (1.0 - diagonal_on)[None] + diagonal_on[None] * reading_numbers[:, :, None]


def draw_cond_cov(key, part):
    key = jax.random.fold_in(key, 23)
    key_base = jax.random.fold_in(key, 1)
    key_diag = jax.random.fold_in(key, 2)
    base = jax.random.truncated_normal(key_base, -4.0, 4.0, (EPOCH_COUNT_ALL, N, N), jnp.float32)
    diag_values = jax.random.uniform(key_diag, (EPOCH_COUNT_ALL, N), jnp.float32, 0.6, 1.6)
    symmetric = (base + jnp.swapaxes(base, 1, 2)) * (0.2 / math.sqrt(2.0 * N))
    diagonal_on = diagonal_mask()
    return 0.05 * (symmetric * (1.0 - diagonal_on)[None] + diagonal_on[None] * diag_values[:, :, None])


def set_ends(array, key, smallest, largest):
    longest = array.shape.index(max(array.shape))
    spots = []
    for shift in (0, 1):
        where = [jax.random.randint(jax.random.fold_in(key, axis), (), 0, length) for axis, length in enumerate(array.shape)]
        where[longest] = (where[longest] + shift) % array.shape[longest]
        spots.append(tuple(where))
    return array.at[spots[0]].set(smallest).at[spots[1]].set(largest)


def level_of(stream_key, dims, shards, low, top_value):
    level, own = 1.0, jax.random.fold_in(stream_key, 6)
    for dim, shards_of in shards:
        steps = jnp.exp(jax.random.uniform(jax.random.fold_in(own, dim), (shards_of,), jnp.float32, low / len(shards), top_value / len(shards)))
        level = level * jnp.repeat(steps, dims[dim] // shards_of).reshape([-1 if axis == dim else 1 for axis in range(len(dims))])
    return level


def noise(key, extent, scale, most, shards=(), dtype=jnp.bfloat16):
    level = level_of(key, extent, shards, -0.22, 0.18) if shards else 1.0
    values = jax.random.normal(key, extent, jnp.float32) * scale * level
    return jnp.minimum(jnp.maximum(values, -most), most).astype(dtype)


def setup_inputs(seed: int = 0) -> dict:
    streams_of = jax.random.split(jax.random.key(seed), 7)
    gain = draw_gain(jax.random.fold_in(streams_of[6], 71), 0)
    cond_cov = draw_cond_cov(jax.random.fold_in(streams_of[6], 71), 0)
    pred_mean = noise(streams_of[2], (EPOCH_COUNT_ALL, N), 0.3, 4.0, ((0, 16), (1, 16)), jnp.float32)
    correction = noise(streams_of[3], (EPOCH_COUNT_ALL, N), 0.3, 4.0, ((0, 16), (1, 16)), jnp.float32)
    spread = jnp.clip(jnp.exp(math.log(0.5) - 2.3025851 * jax.random.uniform(streams_of[4], (N,), jnp.float32) ** level_of(streams_of[4], (N,), ((0, 16),), -0.2, 0.2)), 0.05, 0.5)
    observed = set_ends((jax.random.randint(streams_of[5], (EPOCH_COUNT_ALL, BLOCKS), 0, 4) < 3).astype(jnp.int32), jax.random.fold_in(streams_of[5], 1), 0, 1)
    return dict(gain=gain, cond_cov=cond_cov, pred_mean=pred_mean, correction=correction, spread=spread, observed=observed)


highest = lax.Precision.HIGHEST


def reference(gain, cond_cov, pred_mean, correction, spread, observed):
    block_width = N // BLOCKS
    seen_rows = jnp.repeat(observed.astype(jnp.float32), block_width, axis=1)
    offsets = pred_mean + seen_rows * correction
    retained = (jnp.arange(EPOCH_COUNT_ALL) < EPOCH_COUNT_ALL - 1).astype(jnp.float32)
    transition = gain * retained[:, None, None]
    missing_var = (1.0 - seen_rows) * spread[None, :]

    def backward(carried, element):
        mean_now, cov_now = carried
        trans_now, offset_now, cterm_now, added_now = element
        mean_now = jnp.dot(trans_now, mean_now, precision=highest) + offset_now
        moved_cov = jnp.dot(trans_now, cov_now, precision=highest)
        cov_now = lax.dot_general(moved_cov, trans_now, (((1,), (1,)), ((), ())), precision=highest) + (cterm_now + jnp.diag(added_now))
        return (mean_now, cov_now), (mean_now, cov_now)

    initial = (jnp.zeros((N,), jnp.float32), jnp.zeros((N, N), jnp.float32))
    closing_output, outputs = lax.scan(backward, initial, (transition, offsets, cond_cov, missing_var), reverse=True)
    return outputs[0], outputs[1]
```

```python
import functools
import jax
import jax.numpy as jnp
from jax import lax
from jax.experimental import pallas as pl
from jax.experimental.pallas import tpu as pltpu
from jax.sharding import PartitionSpec as P

F32 = jnp.float32
BF16 = jnp.bfloat16
N = 512
HALF = 256
BAND = 32
X = 4
Y = 4
Z = 8


def split(value):
    high = value.astype(BF16)
    return high, (value - high.astype(F32)).astype(BF16)


def dot(left, right, dims):
    return lax.dot_general(left, right, (dims, ((), ())), preferred_element_type=F32)


def three(left, right, dims):
    (lh, ll), (rh, rl) = left, right
    return dot(lh, rh, dims) + (dot(lh, rl, dims) + dot(ll, rh, dims))


def nn(left, right):
    return three(left, right, ((1,), (0,)))


def nt(left, right):
    return three(left, right, ((1,), (1,)))


def congruence(left, cov, vec, cov_add, vec_add):
    moved = nt(split(cov), left)
    row = nt(split(jnp.concatenate([vec, jnp.zeros_like(vec)], axis=0)), left)[:8]
    return nn(left, split(moved)) + cov_add, row + vec_add


def place():
    t, p = lax.axis_index("tm"), lax.axis_index("panel")
    return t // X, lax.rem(t, X), p // 2, lax.rem(p, 2), p


def call(kernel, out_shape, args, scratch=(), flops=0, name=None):
    size = sum(a.size * a.dtype.itemsize for a in args)
    return pl.pallas_call(
        kernel,
        out_shape=out_shape,
        in_specs=[pl.BlockSpec(memory_space=pltpu.VMEM)] * len(args),
        out_specs=jax.tree.map(lambda _: pl.BlockSpec(memory_space=pltpu.VMEM), out_shape),
        scratch_shapes=list(scratch),
        compiler_params=pltpu.CompilerParams(vmem_limit_bytes=48 * 1024 * 1024),
        cost_estimate=pl.CostEstimate(flops=flops * 6 * N**3, bytes_accessed=size, transcendentals=0),
        name=name,
    )(*args)


def shape(dims, dtype=F32):
    return jax.ShapeDtypeStruct(dims, dtype)


def compose_gain_kernel(mine, other, a0h, a0l, a1h, a1l, b):
    _, _, z, core, _ = place()
    for source, source_core in ((mine, core), (other, 1 - core)):
        for r in range(Z):
            row = pl.multiple_of((2 * lax.rem(z + r, Z) + source_core) * BAND, BAND)
            for high, low, first in ((a0h, a0l, 0), (a1h, a1l, BAND)):
                h, l = split(source[r, first : first + BAND, :])
                high[pl.ds(row, BAND), :] = h
                low[pl.ds(row, BAND), :] = l
    b[...] = nn((a0h[...], a0l[...]), (a1h[...], a1l[...]))


def compose_cov_kernel(packed, a0h, a0l, cov, vec):
    cov1 = jnp.concatenate([packed[i, BAND : 2 * BAND, :] for i in range(16)], axis=0)
    cov0 = jnp.concatenate([packed[i, :BAND, :] for i in range(16)], axis=0)
    pads = packed[0, 2 * BAND :, :]
    for i in range(1, 16):
        pads = pads + packed[i, 2 * BAND :, :]
    vec0 = jnp.broadcast_to(pads[0:1], (8, N))
    vec1 = jnp.broadcast_to(pads[1:2], (8, N))
    cov[...], vec[0:8, :] = congruence((a0h[...], a0l[...]), cov1, vec1, cov0, vec0)
    vec[8:16, :] = vec1


def row_gain_kernel(mine, other, bh, bl, total, ph, plo):
    _, x, _, core, _ = place()
    for source, source_core in ((mine, core), (other, 1 - core)):
        for r in range(X):
            at = lax.rem(x + r, X)
            row = pl.multiple_of(source_core * HALF, HALF)
            h, l = split(source[r])
            bh[at, pl.ds(row, HALF), :] = h
            bl[at, pl.ds(row, HALF), :] = l
    gain = (bh[3], bl[3])

    def keep(k, value):
        @pl.when(x == k)
        def _():
            ph[...], plo[...] = value

    keep(3, gain)
    keep(2, gain)
    gain = split(nn((bh[2], bl[2]), gain))
    keep(1, gain)
    gain = split(nn((bh[1], bl[1]), gain))
    keep(0, gain)
    total[...] = nn((bh[0], bl[0]), gain)


def row_cov_kernel(mine, other, bh, bl, total, total_vec, suffix, suffix_vec, full, vecs):
    _, x, _, core, _ = place()
    for source, source_core in ((mine, core), (other, 1 - core)):
        for r in range(X):
            at = lax.rem(x + r, X)
            row = pl.multiple_of(source_core * HALF, HALF)
            full[at, pl.ds(row, HALF), :] = source[r, :HALF, :]
            vecs[at] = source[r, HALF:, :]
    cov, vec = full[3], vecs[3]

    @pl.when(x >= 2)
    def _():
        suffix[...], suffix_vec[...] = cov, vec

    for k in (2, 1, 0):
        cov, vec = congruence((bh[k], bl[k]), cov, vec, full[k], vecs[k])
        if k:

            @pl.when(x == k - 1)
            def _():
                suffix[...], suffix_vec[...] = cov, vec

    total[...], total_vec[...] = cov, vec


def last_kernel(
    tm, to, cm, co, ph, plo, suffix, suffix_vec, a1h, a1l, b, cov1, cov0, vec01,
    out, means, th, tl, full, vecs, state, state_vec,
):
    y, x, _, core, p = place()
    for source, source_core in ((cm, core), (co, 1 - core)):
        for r in range(Y):
            at = lax.rem(y + r, Y)
            row = pl.multiple_of(source_core * HALF, HALF)
            full[at, pl.ds(row, HALF), :] = source[r, :HALF, :]
            vecs[at] = source[r, HALF:, :]
    for source, source_core in ((tm, core), (to, 1 - core)):
        for r in range(Y):
            at = lax.rem(y + r, Y)
            row = pl.multiple_of(source_core * HALF, HALF)
            h, l = split(source[r])
            th[at, pl.ds(row, HALF), :] = h
            tl[at, pl.ds(row, HALF), :] = l
    here = jnp.where(y == Y - 1, 0.0, 1.0)
    state[...] = full[3] * here
    state_vec[...] = vecs[3] * here
    for k in (2, 1):

        @pl.when(y < k)
        def _():
            state[...], state_vec[...] = congruence(
                (th[k], tl[k]), state[...], state_vec[...], full[k], vecs[k]
            )

    @pl.when(x < X - 1)
    def _():
        state[...], state_vec[...] = congruence(
            (ph[...], plo[...]), state[...], state_vec[...], suffix[...], suffix_vec[...]
        )

    row = pl.multiple_of(p * BAND, BAND)
    bh, bl = split(b[...])
    b0h, b0l = split(b[pl.ds(row, BAND), :])
    bands = (
        jnp.concatenate([a1h[pl.ds(row, BAND), :], b0h], axis=0),
        jnp.concatenate([a1l[pl.ds(row, BAND), :], b0l], axis=0),
    )
    moved = nn(bands, split(state[...]))
    vec = jnp.concatenate([state_vec[...], jnp.zeros((8, N), F32)], axis=0)
    one = nt(split(jnp.concatenate([moved[:BAND], vec], axis=0)), (a1h[...], a1l[...]))
    zero = nt(split(jnp.concatenate([moved[BAND:], vec], axis=0)), (bh, bl))
    out[1] = one[:BAND] + cov1[...]
    out[0] = zero[:BAND] + cov0[pl.ds(row, BAND), :]
    means[0:8, :] = zero[BAND : BAND + 8] + vec01[0:8, :]
    means[8:16, :] = one[BAND : BAND + 8] + vec01[8:16, :]


SWAP = [(p, p ^ 1) for p in range(16)]


def z_perm(k):
    return [(p, ((p // 2 + k) % Z) * 2 + p % 2) for p in range(16)]


def x_perm(k):
    return [(t, (t // X) * X + (t % X + k) % X) for t in range(16)]


def y_perm(k):
    return [(t, ((t // X + k) % Y) * X + t % X) for t in range(16)]


def gather_z(own):
    rows = own.shape[0] // 2
    up, down = [own], [own]
    for _ in range(3):
        up.append(lax.ppermute(up[-1], "panel", z_perm(-1)))
        down.append(lax.ppermute(down[-1], "panel", z_perm(1)))
    far = [
        lax.ppermute(up[3][:rows], "panel", z_perm(-1)),
        lax.ppermute(down[3][rows:], "panel", z_perm(1)),
    ]
    mine = jnp.concatenate(up + far + down[:0:-1], axis=0).reshape(Z, 2 * rows, N)
    return mine, lax.ppermute(mine, "panel", SWAP)


def gather_four(own, perm):
    rows = own.shape[0] // 16 * 8
    above = lax.ppermute(own, "tm", perm(-1))
    below = lax.ppermute(own, "tm", perm(1))
    far = [
        lax.ppermute(above[:rows], "tm", perm(-1)),
        lax.ppermute(below[rows:], "tm", perm(1)),
    ]
    mine = jnp.concatenate([own, above] + far + [below], axis=0).reshape(4, -1, N)
    return mine, lax.ppermute(mine, "panel", SWAP)


def shards(gain, cond_cov, pred_mean, correction, spread, observed):
    t, p = lax.axis_index("tm"), lax.axis_index("panel")
    core = lax.rem(p, 2)
    step = lax.broadcasted_iota(jnp.int32, (2, 1, 1), 0)
    gains = jnp.where(jnp.logical_and(t == 15, step == 1), 0.0, gain).reshape(2 * BAND, N)
    seen = jnp.repeat(observed.astype(F32), 8, axis=1)
    offset = pred_mean + seen * correction
    rows = p * BAND + lax.broadcasted_iota(jnp.int32, (1, BAND, N), 1)
    lanes = lax.broadcasted_iota(jnp.int32, (1, BAND, N), 2)
    missing = ((1.0 - seen) * spread[None, :])[:, :, None]
    covs = cond_cov + jnp.where(rows == lanes, missing, 0.0)
    spots = jnp.where(lax.broadcasted_iota(jnp.int32, (8, N), 1) // BAND == p, 1.0, 0.0)
    vectors = jnp.concatenate([jnp.tile(offset, (1, 16)), jnp.zeros((6, N), F32)], axis=0) * spots
    packed = jnp.concatenate([covs.reshape(2 * BAND, N), vectors], axis=0)
    packed_all = lax.all_gather(packed, "panel", axis=0)
    square, row8, half = shape((N, N)), shape((8, N)), shape((N, N), BF16)

    mine, other = gather_z(gains)
    a0h, a0l, a1h, a1l, b = call(
        compose_gain_kernel, (half, half, half, half, square), (mine, other), flops=1, name="compose_gain"
    )
    own_half = lambda whole: lax.dynamic_slice_in_dim(whole, core * HALF, HALF, 0)
    mine, other = gather_four(own_half(b), x_perm)
    four = shape((4, N, N), BF16)
    bh, bl, total, ph, plo = call(
        row_gain_kernel, (four, four, square, half, half), (mine, other), flops=3, name="row_gain"
    )
    tm, to = gather_four(own_half(total), y_perm)

    cov0, vec01 = call(
        compose_cov_kernel, (square, shape((16, N))), (packed_all, a0h, a0l), flops=2, name="compose_cov"
    )
    mine, other = gather_four(jnp.concatenate([own_half(cov0), vec01[:8]], axis=0), x_perm)
    full = pltpu.VMEM((4, N, N), F32)
    vecs = pltpu.VMEM((4, 8, N), F32)
    cov_total, vec_total, suffix, suffix_vec = call(
        row_cov_kernel, (square, row8, square, row8), (mine, other, bh, bl), (full, vecs), flops=6, name="row_cov"
    )
    cm, co = gather_four(jnp.concatenate([own_half(cov_total), vec_total], axis=0), y_perm)
    out, means = call(
        last_kernel,
        (shape((2, BAND, N)), shape((16, N))),
        (tm, to, cm, co, ph, plo, suffix, suffix_vec, a1h, a1l, b, covs[1], cov0, vec01),
        (
            pltpu.VMEM((4, N, N), BF16), pltpu.VMEM((4, N, N), BF16), full, vecs,
            pltpu.VMEM((N, N), F32), pltpu.VMEM((8, N), F32),
        ),
        flops=7,
        name="last",
    )
    mean = lax.dynamic_slice(means.reshape(2, 8, N)[:, 0, :], (0, p * BAND), (2, BAND))
    return mean, out


def solution(mesh):
    placed = (
        P("tm", "panel", None),
        P("tm", "panel", None),
        P("tm", "panel"),
        P("tm", "panel"),
        P("panel"),
        P("tm", "panel"),
    )
    return jax.shard_map(
        shards,
        mesh=mesh,
        in_specs=placed,
        out_specs=(P("tm", "panel"), P("tm", "panel", None)),
        check_vma=False,
    )
```

```python
import functools
import jax
import jax.numpy as jnp
from jax import lax
from jax.experimental import pallas as pl
from jax.experimental.pallas import tpu as pltpu
from jax.sharding import PartitionSpec as P

F32 = jnp.float32
BF16 = jnp.bfloat16
N = 512
HALF = 256
BAND = 32
X = 4
Y = 4
Z = 8


def split(value):
    high = value.astype(BF16)
    return high, (value - high.astype(F32)).astype(BF16)


def dot(left, right, dims):
    return lax.dot_general(left, right, (dims, ((), ())), preferred_element_type=F32)


def three(left, right, dims):
    (lh, ll), (rh, rl) = left, right
    return dot(lh, rh, dims) + (dot(lh, rl, dims) + dot(ll, rh, dims))


def nn(left, right):
    return three(left, right, ((1,), (0,)))


def nt(left, right):
    return three(left, right, ((1,), (1,)))


def place():
    t, p = lax.axis_index("tm"), lax.axis_index("panel")
    return t // X, lax.rem(t, X), p // 2, lax.rem(p, 2), p


def call(kernel, out_shape, args, scratch=(), flops=0, name=None, space=pltpu.VMEM):
    size = sum(a.size * a.dtype.itemsize for a in args)
    return pl.pallas_call(
        kernel,
        out_shape=out_shape,
        in_specs=[pl.BlockSpec(memory_space=space)] * len(args),
        out_specs=jax.tree.map(lambda _: pl.BlockSpec(memory_space=pltpu.VMEM), out_shape),
        scratch_shapes=list(scratch),
        compiler_params=pltpu.CompilerParams(vmem_limit_bytes=8 * 1024 * 1024),
        cost_estimate=pl.CostEstimate(flops=int(flops * 6 * N**3), bytes_accessed=size, transcendentals=0),
        name=name,
    )(*args)


def shape(dims, dtype=F32):
    return jax.ShapeDtypeStruct(dims, dtype)


def band_kernel(*refs):
    sources, (band, offset), places, arrived = refs[:5], refs[5:7], refs[7:12], refs[12]
    copies = [pltpu.make_async_copy(a, b, arrived.at[i]) for i, (a, b) in enumerate(zip(sources, places))]
    for copy in copies:
        copy.start()
    for copy in copies:
        copy.wait()
    cond_cov, pred_mean, correction, spread, observed = places
    _, _, _, _, p = place()
    block = lax.broadcasted_iota(jnp.int32, (2, BAND), 1) // 8
    seen = jnp.zeros((2, BAND), F32)
    for i in range(4):
        seen = seen + jnp.where(block == i, observed[:, i : i + 1].astype(F32), 0.0)
    value = pred_mean[...] + seen * correction[...]
    missing = (1.0 - seen) * spread[...]
    offset[...] = value
    lane = lax.broadcasted_iota(jnp.int32, (BAND, N), 1) - p * BAND
    diagonal = lane == lax.broadcasted_iota(jnp.int32, (BAND, N), 0)
    own = jnp.logical_and(lane[:8] >= 0, lane[:8] < BAND)
    wide = jnp.concatenate([jnp.concatenate([part] * 16, axis=1) for part in (missing, value)], axis=0)
    band[0:BAND, :] = cond_cov[0] + jnp.where(diagonal, wide[0:1, :], 0.0)
    band[BAND : 2 * BAND, :] = cond_cov[1] + jnp.where(diagonal, wide[1:2, :], 0.0)
    rows = jnp.concatenate([wide[2:4, :], jnp.zeros((6, N), F32)], axis=0)
    band[2 * BAND :, :] = jnp.where(own, rows, 0.0)


def z_pieces(pieces, rows):
    chip, r1, s1, r2, s2, r3, s3, r4, s4 = pieces
    _, _, z, core, _ = place()
    way = 2 * core - 1
    band = lambda away, c: 2 * lax.rem(z + away + Z, Z) + c
    found = [(chip, 0, band(0, core)), (chip, rows, band(0, 1 - core))]
    for i, (r, s) in enumerate(((r1, s1), (r2, s2), (r3, s3)), 1):
        found += [(r, 0, band(way * i, core)), (r, rows, band(way * i, 1 - core))]
        found += [(s, 0, band(-way * i, 1 - core)), (s, rows, band(-way * i, core))]
    return found + [(r4, 0, band(4, core)), (s4, 0, band(4, 1 - core))]


def half_pieces(pieces, at, lead, height):
    r1, s1, r2, s2 = pieces
    _, _, _, core, _ = place()
    way = 2 * core - 1
    near, far = pl.multiple_of(core * height, height), pl.multiple_of((1 - core) * height, height)
    one, two, three_ = lax.rem(at + way + 4, 4), lax.rem(at - way + 4, 4), lax.rem(at + 2, 4)
    return [
        (r1, lead, one, near),
        (r1, lead + height, one, far),
        (s1, lead, two, far),
        (s1, lead + height, two, near),
        (r2, lead, three_, near),
        (s2, lead, three_, far),
    ]


def store_rolled(dest, lead, whole, core, height):
    near, far = pl.multiple_of(core * height, height), pl.multiple_of((1 - core) * height, height)
    dest[lead : lead + height, :] = whole[pl.ds(near, height), :]
    dest[lead + height : lead + 2 * height, :] = whole[pl.ds(far, height), :]


def triangle():
    return (
        lax.broadcasted_iota(jnp.int32, (HALF, HALF), 0) - lax.broadcasted_iota(jnp.int32, (HALF, HALF), 1)
    )


def pack(dest, cov, vec, scratch, core):
    below = triangle()
    last = cov[HALF:, HALF:]
    scratch[:, :HALF] = cov[:HALF, HALF:]
    scratch[:, HALF:] = jnp.where(below >= 0, cov[:HALF, :HALF], last)
    dest[0:1, :] = vec
    dest[1:2, :HALF] = jnp.sum(jnp.where(below == 0, last, 0.0), axis=0, keepdims=True)
    dest[1:2, HALF:] = jnp.zeros((1, HALF), F32)
    dest[2:8, :] = jnp.zeros((6, N), F32)
    store_rolled(dest, 8, scratch, core, HALF // 2)


def unpack(packed, heads, at, store):
    below = triangle()
    side, mixed = packed[at, :, :HALF], packed[at, :, HALF:]
    turned = mixed.T
    store(0, 0, jnp.where(below >= 0, mixed, turned))
    store(0, HALF, side)
    store(HALF, 0, side.T)
    store(HALF, HALF, jnp.where(below < 0, mixed, jnp.where(below == 0, heads[at, 1:2, :HALF], turned)))


def compose_gain_kernel(*refs):
    pieces, (a0h, a0l, a1h, a1l, bh, bl, sent, b) = refs[:9], refs[9:]
    _, _, _, core, _ = place()
    kept = jnp.where(lax.axis_index("tm") == 15, 0.0, 1.0)
    for source, first, band in z_pieces(pieces, 2 * BAND):
        row = pl.multiple_of(band * BAND, BAND)
        a0h[pl.ds(row, BAND), :], a0l[pl.ds(row, BAND), :] = split(source[first : first + BAND, :])
        a1h[pl.ds(row, BAND), :], a1l[pl.ds(row, BAND), :] = split(
            source[first + BAND : first + 2 * BAND, :] * kept
        )
    b[...] = nn((a0h[...], a0l[...]), (a1h[...], a1l[...]))
    bh[...], bl[...] = split(b[...])
    store_rolled(sent, 0, b, core, HALF)


def congruence(left, state, add, add_vec):
    moved = nt(split(state[...]), left)
    state[:N, :] = nn(left, split(moved[:N])) + add
    state[N:, :] = moved[N:] + add_vec


def compose_cov_kernel(*refs):
    pieces, (a0h, a0l, offset), (cov_bands, offsets, sent, state, cov0, scratch) = refs[:9], refs[9:12], refs[12:]
    _, _, _, core, p = place()
    pads = jnp.zeros((8, N), F32)
    for source, first, band in z_pieces(pieces, 2 * BAND + 8):
        row = pl.multiple_of(band * BAND, BAND)
        cov0[pl.ds(row, BAND), :] = source[first : first + BAND, :]
        state[pl.ds(row, BAND), :] = source[first + BAND : first + 2 * BAND, :]
        pads = pads + source[first + 2 * BAND : first + 2 * BAND + 8, :]
    state[N:, :] = jnp.broadcast_to(pads[1:2], (16, N))
    row = pl.multiple_of(p * BAND, BAND)
    cov_bands[BAND:, :] = state[pl.ds(row, BAND), :]
    moved = nt(split(state[N:, :]), (a0h[pl.ds(row, BAND), :], a0l[pl.ds(row, BAND), :]))
    offsets[0:1, :] = moved[0:1] + offset[0:1, :]
    offsets[1:2, :] = offset[1:2, :]
    congruence((a0h[...], a0l[...]), state, cov0[...], jnp.broadcast_to(pads[0:1], (16, N)))
    cov_bands[:BAND, :] = state[pl.ds(row, BAND), :]
    pack(sent, state[:N, :], state[N : N + 1, :], scratch, core)


def row_gain_kernel(ownh, ownl, r1, s1, r2, s2, bh, bl, sent, ph, plo, total):
    _, x, _, core, _ = place()
    bh[x], bl[x] = ownh[...], ownl[...]
    for source, first, at, row in half_pieces((r1, s1, r2, s2), x, 0, HALF):
        bh[at, pl.ds(row, HALF), :], bl[at, pl.ds(row, HALF), :] = split(source[first : first + HALF, :])
    gain = (bh[3], bl[3])

    def keep(k, value):
        @pl.when(x == k)
        def _():
            ph[...], plo[...] = value

    keep(3, gain)
    keep(2, gain)
    gain = split(nn((bh[2], bl[2]), gain))
    keep(1, gain)
    gain = split(nn((bh[1], bl[1]), gain))
    keep(0, gain)
    total[...] = nn((bh[0], bl[0]), gain)
    store_rolled(sent, 0, total, core, HALF)


def row_cov_kernel(
    own, r1, s1, r2, s2, bh, bl, sent, suffix, suffix_vec, packed, heads, cov, state, scratch
):
    _, x, _, core, _ = place()
    near, far = (pl.multiple_of(c * HALF // 2, HALF // 2) for c in (core, 1 - core))
    own_halves = [(own, 8, x, near), (own, 8 + HALF // 2, x, far)]
    for source, first, at, row in own_halves + half_pieces((r1, s1, r2, s2), x, 8, HALF // 2):
        packed[at, pl.ds(row, HALF // 2), :] = source[first : first + HALF // 2, :]
        heads[at] = source[0:8, :]
    vecs = lambda k: jnp.broadcast_to(heads[k, 0:1, :], (16, N))

    def into(dest):
        def store(row, column, value):
            dest[row : row + HALF, column : column + HALF] = value

        return store

    unpack(packed, heads, 3, into(state))
    state[N:, :] = vecs(3)

    @pl.when(x >= 2)
    def _():
        suffix[...], suffix_vec[...] = state[:N, :], state[N : N + 8, :]

    for k in (2, 1, 0):
        unpack(packed, heads, k, into(cov))
        congruence((bh[k], bl[k]), state, cov[...], vecs(k))
        if k:

            @pl.when(x == k - 1)
            def _():
                suffix[...], suffix_vec[...] = state[:N, :], state[N : N + 8, :]

    pack(sent, state[:N, :], state[N : N + 1, :], scratch, core)


def ready_kernel(
    r1, s1, r2, s2, a1h, a1l, bh, bl, ph, plo, suffix, suffix_vec,
    th, tl, lefth, leftl, base, base_mean,
):
    y, x, _, _, p = place()
    for source, first, at, row in half_pieces((r1, s1, r2, s2), y, 0, HALF):

        @pl.when(jnp.logical_or(at == 1, at == 2))
        def _():
            slot = at - 1
            th[slot, pl.ds(row, HALF), :], tl[slot, pl.ds(row, HALF), :] = split(source[first : first + HALF, :])

    row = pl.multiple_of(p * BAND, BAND)
    band = tuple(
        jnp.concatenate([one[pl.ds(row, BAND), :], zero[pl.ds(row, BAND), :]], axis=0)
        for one, zero in ((a1h, bh), (a1l, bl))
    )
    lefth[...] = jnp.zeros_like(lefth)
    leftl[...] = jnp.zeros_like(leftl)
    lefth[3], leftl[3] = band
    base[...] = jnp.zeros_like(base)
    base_mean[...] = jnp.zeros_like(base_mean)

    @pl.when(x < X - 1)
    def _():
        base[...] = nn(band, split(suffix[...]))
        base_mean[...] = nt(split(jnp.concatenate([suffix_vec[...], suffix_vec[...]], axis=0)), band)
        lefth[3], leftl[3] = split(nn(band, (ph[...], plo[...])))

    for k in (0, 1, 2):

        @pl.when(y == k)
        def _():
            now = (lefth[3], leftl[3])
            lefth[k], leftl[k] = now
            for j in range(k, 2):
                now = split(nn(now, (th[j], tl[j])))
                lefth[j + 1], leftl[j + 1] = now


def last_kernel(
    r1, s1, r2, s2, th, tl, lefth, leftl, base, base_mean, ph, plo, a1h, a1l, bh, bl, cov_bands, offsets,
    mean, out, packed, heads, dh, dl, moved, row_mean,
):
    y, x, _, _, _ = place()
    for source, first, at, row in half_pieces((r1, s1, r2, s2), y, 8, HALF // 2):
        packed[at, pl.ds(row, HALF // 2), :] = source[first : first + HALF // 2, :]
        heads[at] = source[0:8, :]
    moved[...] = jnp.zeros_like(moved)
    row_mean[...] = base_mean[...]
    for k in (2, 1, 0):

        @pl.when(y <= k)
        def _():
            def store(row, column, value):
                place_ = (slice(row, row + HALF), slice(column, column + HALF))
                dh[place_], dl[place_] = split(value)

            unpack(packed, heads, k + 1, store)
            left = (lefth[k], leftl[k])
            moved[...] += nn(left, (dh[...], dl[...]))
            row_mean[...] += nt(split(jnp.broadcast_to(heads[k + 1, 0:1, :], (16, N))), left)

        if k:

            @pl.when(y < k)
            def _():
                moved[...] = nt(split(moved[...]), (th[k - 1], tl[k - 1]))

    @pl.when(x < X - 1)
    def _():
        moved[...] = nt(split(moved[...]), (ph[...], plo[...])) + base[...]

    out[1] = nt(split(moved[:BAND, :]), (a1h[...], a1l[...])) + cov_bands[BAND:, :]
    out[0] = nt(split(moved[BAND:, :]), (bh[...], bl[...])) + cov_bands[:BAND, :]
    mean[1:2, :] = row_mean[0:1, :BAND] + offsets[1:2, :]
    mean[0:1, :] = row_mean[0:1, BAND : 2 * BAND] + offsets[0:1, :]


def device(y, x, z, core):
    return ((y % Y) * X + x % X) * 16 + (z % Z) * 2 + core


def perm(dy, dx, dz):
    return [
        (device(y, x, z, c), device(y + (1 - 2 * c) * dy, x + (1 - 2 * c) * dx, z + (1 - 2 * c) * dz, c))
        for y in range(Y)
        for x in range(X)
        for z in range(Z)
        for c in range(2)
    ]


AXES = ("tm", "panel")
ROUND_Y, ROUND_X, ROUND_Z = perm(1, 0, 0), perm(0, 1, 0), perm(0, 0, 1)
SWAP = [(i, i ^ 1) for i in range(256)]


def swap(piece):
    return lax.ppermute(piece, AXES, SWAP)


def gather_z(first, second):
    turns = [Turn(first), Turn(second)]
    for _ in range(4):
        for turn in turns:
            turn.go()
    return [turn.finish() for turn in turns]


class Turn:
    def __init__(self, own):
        self.rows, self.hop, self.pieces = own.shape[0], 0, []
        self.now = jnp.concatenate([own, swap(own)], axis=0)

    def go(self):
        self.pieces += [self.now, swap(self.now)] if self.hop else [self.now]
        self.hop += 1
        self.now = hop(self.now if self.hop < 4 else self.now[: self.rows], ROUND_Z)

    def finish(self):
        return [*self.pieces, self.now, swap(self.now)]


def together(*values):
    return lax.optimization_barrier(values)


def after(value, *others):
    return together(value, *others)[0]


def hop(sent, way):
    return lax.ppermute(sent, AXES, way)


def first_half(sent):
    return sent[: (sent.shape[0] + 8) // 16 * 8]


def shards(gain, cond_cov, pred_mean, correction, spread, observed):
    square, row8, half = shape((N, N)), shape((8, N)), shape((N, N), BF16)
    args = (cond_cov, pred_mean, correction, spread[None, :], observed)
    band, offset = call(
        band_kernel,
        (shape((2 * BAND + 8, N)), shape((2, BAND))),
        args,
        (*[pltpu.VMEM(a.shape, a.dtype) for a in args], pltpu.SemaphoreType.DMA((5,))),
        name="band",
        space=pltpu.HBM,
    )
    a_pieces, c_pieces = gather_z(gain.reshape(2 * BAND, N), band)
    a0h, a0l, a1h, a1l, b0h, b0l, sent = call(
        compose_gain_kernel,
        (half, half, half, half, half, half, square),
        a_pieces,
        (pltpu.VMEM((N, N), F32),),
        flops=1,
        name="compose_gain",
    )
    b1 = hop(sent, ROUND_X)
    state = pltpu.VMEM((N + 16, N), F32)
    scratch = pltpu.VMEM((HALF, N), F32)
    packed_four = (pltpu.VMEM((4, HALF, N), F32), pltpu.VMEM((4, 8, N), F32))
    cov_bands, offsets, c0 = call(
        compose_cov_kernel,
        (shape((2 * BAND, N)), shape((2, BAND)), shape((HALF + 8, N))),
        (*c_pieces, a0h, a0l, offset),
        (state, pltpu.VMEM((N, N), F32), scratch),
        flops=2,
        name="compose_cov",
    )
    b1, c1 = together(b1, hop(c0, ROUND_X))
    b_near, c_near = swap(b1), swap(c1)
    b2, c2 = together(hop(first_half(b1), ROUND_X), hop(first_half(c1), ROUND_X))
    b_pieces, c_pieces = (b1, b_near, b2, swap(b2)), (c1, c_near, c2, swap(c2))
    four = shape((4, N, N), BF16)
    bh, bl, sent, ph, plo = call(
        row_gain_kernel,
        (four, four, square, half, half),
        (b0h, b0l, *b_pieces),
        (pltpu.VMEM((N, N), F32),),
        flops=3,
        name="row_gain",
    )
    t1 = hop(sent, ROUND_Y)
    sent, suffix, suffix_vec = call(
        row_cov_kernel,
        (shape((HALF + 8, N)), square, row8),
        (c0, *c_pieces, bh, bl),
        (*packed_four, pltpu.VMEM((N, N), F32), state, scratch),
        flops=6,
        name="row_cov",
    )
    t1, d1 = together(t1, hop(sent, ROUND_Y))
    t_near, d_near = swap(t1), swap(d1)
    t2, d2 = together(hop(first_half(t1), ROUND_Y), hop(first_half(d1), ROUND_Y))
    t_pieces, d_pieces = (t1, t_near, t2, swap(t2)), (d1, d_near, d2, swap(d2))
    band, two = shape((4, 2 * BAND, N), BF16), shape((2, N, N), BF16)
    ready = call(
        ready_kernel,
        (two, two, band, band, shape((2 * BAND, N)), shape((16, 2 * BAND))),
        (*t_pieces, a1h, a1l, b0h, b0l, ph, plo, suffix, suffix_vec),
        flops=1,
        name="ready",
    )
    return call(
        last_kernel,
        (shape((2, BAND)), shape((2, BAND, N))),
        (*d_pieces, *ready, ph, plo, a1h, a1l, b0h, b0l, cov_bands, offsets),
        (
            *packed_four, pltpu.VMEM((N, N), BF16), pltpu.VMEM((N, N), BF16),
            pltpu.VMEM((2 * BAND, N), F32), pltpu.VMEM((16, 2 * BAND), F32),
        ),
        flops=1,
        name="last",
    )


def solution(mesh):
    placed = (
        P("tm", "panel", None),
        P("tm", "panel", None),
        P("tm", "panel"),
        P("tm", "panel"),
        P("panel"),
        P("tm", "panel"),
    )
    return jax.shard_map(
        shards,
        mesh=mesh,
        in_specs=placed,
        out_specs=(P("tm", "panel"), P("tm", "panel", None)),
        check_vma=False,
    )
```

```python
import functools
import jax
import jax.numpy as jnp
from jax import lax
from jax.experimental import pallas as pl
from jax.experimental.pallas import tpu as pltpu
from jax.sharding import PartitionSpec as P

F32 = jnp.float32
BF16 = jnp.bfloat16
N = 512
HALF = 256
BAND = 32
X = 4
Y = 4
Z = 8


def split(value):
    high = value.astype(BF16)
    return high, (value - high.astype(F32)).astype(BF16)


def dot(left, right, dims):
    return lax.dot_general(left, right, (dims, ((), ())), preferred_element_type=F32)


def three(left, right, dims):
    (lh, ll), (rh, rl) = left, right
    return dot(lh, rh, dims) + (dot(lh, rl, dims) + dot(ll, rh, dims))


def few(left, right, dims):
    (lh, ll), (rh, rl) = left, right
    rows = lh.shape[0]
    both = dot(jnp.concatenate([lh, ll], axis=0), rh, dims)
    return both[:rows] + (both[rows:] + dot(lh, rl, dims))


def few_nn(left, right):
    return few(left, right, ((1,), (0,)))


def few_nt(left, right):
    return few(left, right, ((1,), (1,)))


def nn(left, right):
    return three(left, right, ((1,), (0,)))


def nt(left, right):
    return three(left, right, ((1,), (1,)))


def place():
    t, p = lax.axis_index("tm"), lax.axis_index("panel")
    return t // X, lax.rem(t, X), p // 2, lax.rem(p, 2), p


def call(kernel, out_shape, args, scratch=(), flops=0, name=None, space=pltpu.VMEM, light=False):
    size = 0 if light else sum(a.size * a.dtype.itemsize for a in args)
    return pl.pallas_call(
        kernel,
        out_shape=out_shape,
        in_specs=[pl.BlockSpec(memory_space=space)] * len(args),
        out_specs=jax.tree.map(lambda _: pl.BlockSpec(memory_space=pltpu.VMEM), out_shape),
        scratch_shapes=list(scratch),
        compiler_params=pltpu.CompilerParams(vmem_limit_bytes=8 * 1024 * 1024),
        cost_estimate=pl.CostEstimate(flops=int(flops * 6 * N**3), bytes_accessed=size, transcendentals=0),
        name=name,
    )(*args)


def shape(dims, dtype=F32):
    return jax.ShapeDtypeStruct(dims, dtype)


def band_kernel(*refs):
    sources, (band, offset), places, arrived = refs[:5], refs[5:7], refs[7:12], refs[12]
    copies = [pltpu.make_async_copy(a, b, arrived.at[i]) for i, (a, b) in enumerate(zip(sources, places))]
    for copy in copies:
        copy.start()
    for copy in copies:
        copy.wait()
    cond_cov, pred_mean, correction, spread, observed = places
    _, _, _, _, p = place()
    block = lax.broadcasted_iota(jnp.int32, (2, BAND), 1) // 8
    seen = jnp.zeros((2, BAND), F32)
    for i in range(4):
        seen = seen + jnp.where(block == i, observed[:, i : i + 1].astype(F32), 0.0)
    value = pred_mean[...] + seen * correction[...]
    missing = (1.0 - seen) * spread[...]
    offset[...] = value
    lane = lax.broadcasted_iota(jnp.int32, (BAND, N), 1) - p * BAND
    diagonal = lane == lax.broadcasted_iota(jnp.int32, (BAND, N), 0)
    own = jnp.logical_and(lane[:8] >= 0, lane[:8] < BAND)
    wide = jnp.concatenate([jnp.concatenate([part] * 16, axis=1) for part in (missing, value)], axis=0)
    band[0:BAND, :] = cond_cov[0] + jnp.where(diagonal, wide[0:1, :], 0.0)
    band[BAND : 2 * BAND, :] = cond_cov[1] + jnp.where(diagonal, wide[1:2, :], 0.0)
    rows = jnp.concatenate([wide[2:4, :], jnp.zeros((6, N), F32)], axis=0)
    band[2 * BAND :, :] = jnp.where(own, rows, 0.0)


def z_pieces(pieces, rows):
    chip, r1, s1, r2, s2, r3, s3, r4, s4 = pieces
    _, _, z, core, _ = place()
    way = 2 * core - 1
    band = lambda away, c: 2 * lax.rem(z + away + Z, Z) + c
    found = [(chip, 0, band(0, core)), (chip, rows, band(0, 1 - core))]
    for i, (r, s) in enumerate(((r1, s1), (r2, s2), (r3, s3)), 1):
        found += [(r, 0, band(way * i, core)), (r, rows, band(way * i, 1 - core))]
        found += [(s, 0, band(-way * i, 1 - core)), (s, rows, band(-way * i, core))]
    return found + [(r4, 0, band(4, core)), (s4, 0, band(4, 1 - core))]


def half_pieces(pieces, at, lead, height):
    r1, s1, r2, s2 = pieces
    _, _, _, core, _ = place()
    way = 2 * core - 1
    near, far = pl.multiple_of(core * height, height), pl.multiple_of((1 - core) * height, height)
    one, two, three_ = lax.rem(at + way + 4, 4), lax.rem(at - way + 4, 4), lax.rem(at + 2, 4)
    return [
        (r1, lead, one, near),
        (r1, lead + height, one, far),
        (s1, lead, two, far),
        (s1, lead + height, two, near),
        (r2, lead, three_, near),
        (s2, lead, three_, far),
    ]


def store_rolled(dest, lead, whole, core, height):
    near, far = pl.multiple_of(core * height, height), pl.multiple_of((1 - core) * height, height)
    dest[lead : lead + height, :] = whole[pl.ds(near, height), :]
    dest[lead + height : lead + 2 * height, :] = whole[pl.ds(far, height), :]


def triangle():
    return (
        lax.broadcasted_iota(jnp.int32, (HALF, HALF), 0) - lax.broadcasted_iota(jnp.int32, (HALF, HALF), 1)
    )


def pack(dest, cov, vec, scratch, core):
    below = triangle()
    last = cov[HALF:, HALF:]
    scratch[:, :HALF] = cov[:HALF, HALF:]
    scratch[:, HALF:] = jnp.where(below >= 0, cov[:HALF, :HALF], last)
    dest[0:1, :] = vec
    dest[1:2, :HALF] = jnp.sum(jnp.where(below == 0, last, 0.0), axis=0, keepdims=True)
    dest[1:2, HALF:] = jnp.zeros((1, HALF), F32)
    dest[2:8, :] = jnp.zeros((6, N), F32)
    store_rolled(dest, 8, scratch, core, HALF // 2)


def unpack(packed, heads, at, store):
    below = triangle()
    side, mixed = packed[at, :, :HALF], packed[at, :, HALF:]
    turned = mixed.T
    store(0, 0, jnp.where(below >= 0, mixed, turned))
    store(0, HALF, side)
    store(HALF, 0, side.T)
    store(HALF, HALF, jnp.where(below < 0, mixed, jnp.where(below == 0, heads[at, 1:2, :HALF], turned)))


def compose_gain_kernel(*refs):
    pieces, (a0h, a0l, a1h, a1l, bh, bl, sent, b) = refs[:9], refs[9:]
    _, _, _, core, _ = place()
    kept = jnp.where(lax.axis_index("tm") == 15, 0.0, 1.0)
    for source, first, band in z_pieces(pieces, 2 * BAND):
        row = pl.multiple_of(band * BAND, BAND)
        a0h[pl.ds(row, BAND), :], a0l[pl.ds(row, BAND), :] = split(source[first : first + BAND, :])
        a1h[pl.ds(row, BAND), :], a1l[pl.ds(row, BAND), :] = split(
            source[first + BAND : first + 2 * BAND, :] * kept
        )
    b[...] = nn((a0h[...], a0l[...]), (a1h[...], a1l[...]))
    bh[...], bl[...] = split(b[...])
    store_rolled(sent, 0, b, core, HALF)


def congruence(left, state, add, add_vec):
    moved = nt(split(state[...]), left)
    state[:N, :] = nn(left, split(moved[:N])) + add
    state[N:, :] = moved[N:] + add_vec


def compose_cov_kernel(*refs):
    pieces, (a0h, a0l, offset), (cov_bands, offsets, sent, state, cov0, scratch) = refs[:9], refs[9:12], refs[12:]
    _, _, _, core, p = place()
    pads = jnp.zeros((8, N), F32)
    for source, first, band in z_pieces(pieces, 2 * BAND + 8):
        row = pl.multiple_of(band * BAND, BAND)
        cov0[pl.ds(row, BAND), :] = source[first : first + BAND, :]
        state[pl.ds(row, BAND), :] = source[first + BAND : first + 2 * BAND, :]
        pads = pads + source[first + 2 * BAND : first + 2 * BAND + 8, :]
    state[N:, :] = jnp.broadcast_to(pads[1:2], (16, N))
    row = pl.multiple_of(p * BAND, BAND)
    cov_bands[BAND:, :] = state[pl.ds(row, BAND), :]
    moved = nt(split(state[N:, :]), (a0h[pl.ds(row, BAND), :], a0l[pl.ds(row, BAND), :]))
    offsets[0:1, :] = moved[0:1] + offset[0:1, :]
    offsets[1:2, :] = offset[1:2, :]
    congruence((a0h[...], a0l[...]), state, cov0[...], jnp.broadcast_to(pads[0:1], (16, N)))
    cov_bands[:BAND, :] = state[pl.ds(row, BAND), :]
    pack(sent, state[:N, :], state[N : N + 1, :], scratch, core)


def row_gain_kernel(ownh, ownl, r1, s1, r2, s2, bh, bl, sent, ph, plo, total):
    _, x, _, core, _ = place()
    bh[x], bl[x] = ownh[...], ownl[...]
    for source, first, at, row in half_pieces((r1, s1, r2, s2), x, 0, HALF):
        bh[at, pl.ds(row, HALF), :], bl[at, pl.ds(row, HALF), :] = split(source[first : first + HALF, :])
    gain = (bh[3], bl[3])

    def keep(k, value):
        @pl.when(x == k)
        def _():
            ph[...], plo[...] = value

    keep(3, gain)
    keep(2, gain)
    gain = split(nn((bh[2], bl[2]), gain))
    keep(1, gain)
    gain = split(nn((bh[1], bl[1]), gain))
    keep(0, gain)
    total[...] = nn((bh[0], bl[0]), gain)
    store_rolled(sent, 0, total, core, HALF)


def row_cov_kernel(
    own, r1, s1, r2, s2, bh, bl, sent, suffix, suffix_vec, packed, heads, cov, state, scratch
):
    _, x, _, core, _ = place()
    near, far = (pl.multiple_of(c * HALF // 2, HALF // 2) for c in (core, 1 - core))
    own_halves = [(own, 8, x, near), (own, 8 + HALF // 2, x, far)]
    for source, first, at, row in own_halves + half_pieces((r1, s1, r2, s2), x, 8, HALF // 2):
        packed[at, pl.ds(row, HALF // 2), :] = source[first : first + HALF // 2, :]
        heads[at] = source[0:8, :]
    vecs = lambda k: jnp.broadcast_to(heads[k, 0:1, :], (16, N))

    def into(dest):
        def store(row, column, value):
            dest[row : row + HALF, column : column + HALF] = value

        return store

    unpack(packed, heads, 3, into(state))
    state[N:, :] = vecs(3)

    @pl.when(x >= 2)
    def _():
        suffix[...], suffix_vec[...] = state[:N, :], state[N : N + 8, :]

    for k in (2, 1, 0):
        unpack(packed, heads, k, into(cov))
        congruence((bh[k], bl[k]), state, cov[...], vecs(k))
        if k:

            @pl.when(x == k - 1)
            def _():
                suffix[...], suffix_vec[...] = state[:N, :], state[N : N + 8, :]

    pack(sent, state[:N, :], state[N : N + 1, :], scratch, core)


def mirrored(packed, heads, high, low):
    def store(row, column, value):
        at = (slice(row, row + HALF), slice(column, column + HALF))
        high[at], low[at] = split(value)

    unpack(packed, heads, 0, store)


def mean_of(head, left):
    return few_nt(split(jnp.broadcast_to(head, (16, N))), left)


def own_kernel(a1h, a1l, bh, bl, ph, plo, suffix, suffix_vec, vh, vl, base, mean):
    _, x, _, _, p = place()
    row = pl.multiple_of(p * BAND, BAND)
    band = tuple(
        jnp.concatenate([one[pl.ds(row, BAND), :], zero[pl.ds(row, BAND), :]], axis=0)
        for one, zero in ((a1h, bh), (a1l, bl))
    )
    vh[...], vl[...] = band
    base[...] = jnp.zeros_like(base)
    mean[...] = jnp.zeros_like(mean)

    @pl.when(x < X - 1)
    def _():
        base[...] = few_nn(band, split(suffix[...]))
        mean[...] = mean_of(suffix_vec[0:1, :], band)
        vh[...], vl[...] = split(few_nn(band, (ph[...], plo[...])))


def above_kernel(t1, ts, vh, vl, th, tl, wh, wl):
    y, _, _, core, _ = place()
    for mine, source in ((0, ts), (1, t1)):

        @pl.when(jnp.logical_and(core == mine, y < 2))
        def _():
            th[HALF:, :], tl[HALF:, :] = split(source[:HALF, :])
            th[:HALF, :], tl[:HALF, :] = split(source[HALF:, :])
            wh[...], wl[...] = split(few_nn((vh[...], vl[...]), (th[...], tl[...])))


def near_kernel(d1, ds, vh, vl, mean_in, belowh, belowl, below_vec, near, mean, packed, heads, dh, dl):
    y, _, _, core, _ = place()
    near[...] = jnp.zeros_like(near)
    mean[...] = mean_in[...]
    quarter = HALF // 2

    def take(source, first):
        packed[0, first * quarter : (first + 1) * quarter, :] = source[8 : 8 + quarter, :]
        packed[0, (1 - first) * quarter : (2 - first) * quarter, :] = source[8 + quarter :, :]
        heads[0] = source[0:8, :]

    for mine, above, below in ((0, ds, d1), (1, d1, ds)):

        @pl.when(jnp.logical_and(core == mine, y < 3))
        def _():
            take(above, 1)
            mirrored(packed, heads, dh, dl)
            near[...] = few_nn((vh[...], vl[...]), (dh[...], dl[...]))
            mean[...] += mean_of(heads[0, 0:1, :], (vh[...], vl[...]))

        @pl.when(jnp.logical_and(core == mine, y == 0))
        def _():
            take(below, 0)
            mirrored(packed, heads, belowh, belowl)
            below_vec[...] = heads[0]


def middle_kernel(t2, ts, wh, wl, belowh, belowl, below_vec, mean, beyond, mean_out, th, tl):
    y, _, _, core, _ = place()
    beyond[...] = jnp.zeros_like(beyond)
    mean_out[...] = mean[...]

    @pl.when(y == 0)
    def _():
        mine, its = (pl.multiple_of(c * HALF, HALF) for c in (core, 1 - core))
        th[pl.ds(mine, HALF), :], tl[pl.ds(mine, HALF), :] = split(t2[...])
        th[pl.ds(its, HALF), :], tl[pl.ds(its, HALF), :] = split(ts[...])
        far = (th[...], tl[...])
        left = split(few_nn((wh[...], wl[...]), far))
        mean_out[...] += mean_of(below_vec[0:1, :], left)
        beyond[...] = few_nt(split(few_nn(left, (belowh[...], belowl[...]))), far)


def last_kernel(
    d2, ds, beyond, near, base, mean_in, wh, wl, th, tl, ph, plo, a1h, a1l, bh, bl, cov_bands, offsets,
    mean, out, packed, heads, dh, dl, moved, row_mean,
):
    y, x, _, core, _ = place()
    moved[...] = near[...]
    row_mean[...] = mean_in[...]

    @pl.when(y < 2)
    def _():
        quarter = HALF // 2
        packed[0, pl.ds(pl.multiple_of(core * quarter, quarter), quarter), :] = d2[8:, :]
        packed[0, pl.ds(pl.multiple_of((1 - core) * quarter, quarter), quarter), :] = ds[8:, :]
        heads[0] = d2[0:8, :]
        mirrored(packed, heads, dh, dl)
        left = (wh[...], wl[...])
        row_mean[...] += mean_of(heads[0, 0:1, :], left)
        past = few_nn(left, (dh[...], dl[...])) + beyond[...]
        moved[...] += few_nt(split(past), (th[...], tl[...]))

    @pl.when(x < X - 1)
    def _():
        moved[...] = few_nt(split(moved[...]), (ph[...], plo[...])) + base[...]

    out[1] = few_nt(split(moved[:BAND, :]), (a1h[...], a1l[...])) + cov_bands[BAND:, :]
    out[0] = few_nt(split(moved[BAND:, :]), (bh[...], bl[...])) + cov_bands[:BAND, :]
    mean[1:2, :] = row_mean[0:1, :BAND] + offsets[1:2, :]
    mean[0:1, :] = row_mean[0:1, BAND : 2 * BAND] + offsets[0:1, :]


def device(y, x, z, core):
    return ((y % Y) * X + x % X) * 16 + (z % Z) * 2 + core


def perm(dy, dx, dz):
    return [
        (device(y, x, z, c), device(y + (1 - 2 * c) * dy, x + (1 - 2 * c) * dx, z + (1 - 2 * c) * dz, c))
        for y in range(Y)
        for x in range(X)
        for z in range(Z)
        for c in range(2)
    ]


AXES = ("tm", "panel")
ROUND_Y, ROUND_X, ROUND_Z = perm(1, 0, 0), perm(0, 1, 0), perm(0, 0, 1)
SWAP = [(i, i ^ 1) for i in range(256)]


def swap(piece):
    return lax.ppermute(piece, AXES, SWAP)


def gather_z(first, second):
    turns = [first, second]
    for _ in range(4):
        for turn in turns:
            turn.go()
    return [turn.finish() for turn in turns]


class Turn:
    def __init__(self, own):
        self.rows, self.hop, self.pieces = own.shape[0], 0, []
        self.near = swap(own)
        self.now = jnp.concatenate([own, self.near], axis=0)

    def go(self):
        self.pieces += [self.now, swap(self.now)] if self.hop else [self.now]
        self.hop += 1
        self.now = hop(self.now if self.hop < 4 else self.now[: self.rows], ROUND_Z)

    def finish(self):
        return [*self.pieces, self.now, swap(self.now)]


def together(*values):
    return lax.optimization_barrier(values)


def after(value, *others):
    return together(value, *others)[0]


def hop(sent, way):
    return lax.ppermute(sent, AXES, way)


def first_half(sent):
    return sent[: (sent.shape[0] + 8) // 16 * 8]


def shards(gain, cond_cov, pred_mean, correction, spread, observed):
    square, row8, half = shape((N, N)), shape((8, N)), shape((N, N), BF16)
    first = Turn(gain.reshape(2 * BAND, N))
    args = (cond_cov, pred_mean, correction, spread[None, :], observed)
    band, offset = call(
        band_kernel,
        (shape((2 * BAND + 8, N)), shape((2, BAND))),
        args,
        (*[pltpu.VMEM(a.shape, a.dtype) for a in args[:5]], pltpu.SemaphoreType.DMA((5,))),
        name="band",
        space=pltpu.HBM,
    )
    a_pieces, c_pieces = gather_z(first, Turn(band))
    a0h, a0l, a1h, a1l, b0h, b0l, sent = call(
        compose_gain_kernel,
        (half, half, half, half, half, half, square),
        a_pieces,
        (pltpu.VMEM((N, N), F32),),
        flops=1,
        name="compose_gain",
    )
    b1 = hop(sent, ROUND_X)
    state = pltpu.VMEM((N + 16, N), F32)
    scratch = pltpu.VMEM((HALF, N), F32)
    packed_four = (pltpu.VMEM((4, HALF, N), F32), pltpu.VMEM((4, 8, N), F32))
    cov_bands, offsets, c0 = call(
        compose_cov_kernel,
        (shape((2 * BAND, N)), shape((2, BAND)), shape((HALF + 8, N))),
        (*c_pieces, a0h, a0l, offset),
        (state, pltpu.VMEM((N, N), F32), scratch),
        flops=9,
        name="compose_cov",
    )
    c1 = hop(c0, ROUND_X)
    b2, c2 = hop(first_half(after(b1, offsets)), ROUND_X), hop(first_half(c1), ROUND_X)
    c_near, c_far = swap(c1), swap(c2)
    b_pieces, c_pieces = (b1, swap(b1), b2, after(swap(b2), c_near)), (c1, c_near, c2, c_far)
    four = shape((4, N, N), BF16)
    bh, bl, sent, ph, plo = call(
        row_gain_kernel,
        (four, four, square, half, half),
        (b0h, b0l, *b_pieces),
        (pltpu.VMEM((N, N), F32),),
        name="row_gain",
        light=True,
    )
    t1 = hop(after(sent, c2), ROUND_Y)
    sent, suffix, suffix_vec = call(
        row_cov_kernel,
        (shape((HALF + 8, N)), square, row8),
        (c0, *c_pieces, bh, bl),
        (*packed_four, pltpu.VMEM((N, N), F32), state, scratch),
        flops=6,
        name="row_cov",
    )
    d1 = hop(sent, ROUND_Y)
    rows, vecs = shape((2 * BAND, N), BF16), shape((16, 2 * BAND))
    plain = shape((2 * BAND, N))
    one_packed = (pltpu.VMEM((1, HALF, N), F32), pltpu.VMEM((1, 8, N), F32))
    whole = (pltpu.VMEM((N, N), BF16), pltpu.VMEM((N, N), BF16))
    vh, vl, base, mean = call(
        own_kernel,
        (rows, rows, plain, vecs),
        (a1h, a1l, b0h, b0l, ph, plo, suffix, suffix_vec),
        flops=1,
        name="own",
    )
    t2 = hop(first_half(after(t1, mean)), ROUND_Y)
    t_near, d_near = swap(after(t1, base)), swap(d1)
    th, tl, wh, wl = call(
        above_kernel, (half, half, rows, rows), (t1, t_near, vh, vl), flops=1, name="above"
    )
    d2 = hop(first_half(d1), ROUND_Y)
    belowh, belowl, below_vec, near, mean = call(
        near_kernel,
        (half, half, row8, plain, vecs),
        (d1, d_near, vh, vl, mean),
        (*one_packed, *whole),
        flops=1,
        name="near",
    )
    t_far, d_far = swap(after(t2, d2)), swap(d2)
    beyond, mean = call(
        middle_kernel,
        (plain, vecs),
        (t2, t_far, wh, wl, belowh, belowl, below_vec, mean),
        whole,
        flops=2,
        name="middle",
    )
    return call(
        last_kernel,
        (shape((2, BAND)), shape((2, BAND, N))),
        (d2, d_far, beyond, near, base, mean, wh, wl, th, tl, ph, plo, a1h, a1l, b0h, b0l, cov_bands, offsets),
        (*one_packed, *whole, pltpu.VMEM((2 * BAND, N), F32), pltpu.VMEM((16, 2 * BAND), F32)),
        flops=1,
        name="last",
    )


def solution(mesh):
    placed = (
        P("tm", "panel", None),
        P("tm", "panel", None),
        P("tm", "panel"),
        P("tm", "panel"),
        P("panel"),
        P("tm", "panel"),
    )
    return jax.shard_map(
        shards,
        mesh=mesh,
        in_specs=placed,
        out_specs=(P("tm", "panel"), P("tm", "panel", None)),
        check_vma=False,
    )
```

```python
import functools
import jax
import jax.numpy as jnp
from jax import lax
from jax.experimental import pallas as pl
from jax.experimental.pallas import tpu as pltpu
from jax.sharding import PartitionSpec as P

F32 = jnp.float32
BF16 = jnp.bfloat16
N = 512
HALF = 256
BAND = 32
X = 4
Y = 4
Z = 8


def split(value):
    high = value.astype(BF16)
    return high, (value - high.astype(F32)).astype(BF16)


def dot(left, right, dims):
    return lax.dot_general(left, right, (dims, ((), ())), preferred_element_type=F32)


def three(left, right, dims):
    (lh, ll), (rh, rl) = left, right
    return dot(lh, rh, dims) + (dot(lh, rl, dims) + dot(ll, rh, dims))


def few(left, right, dims):
    (lh, ll), (rh, rl) = left, right
    rows = lh.shape[0]
    both = dot(jnp.concatenate([lh, ll], axis=0), rh, dims)
    return both[:rows] + (both[rows:] + dot(lh, rl, dims))


def few_nn(left, right):
    return few(left, right, ((1,), (0,)))


def few_nt(left, right):
    return few(left, right, ((1,), (1,)))


def nn(left, right):
    return three(left, right, ((1,), (0,)))


def nt(left, right):
    return three(left, right, ((1,), (1,)))


def place():
    t, p = lax.axis_index("tm"), lax.axis_index("panel")
    return t // X, lax.rem(t, X), p // 2, lax.rem(p, 2), p


def call(kernel, out_shape, args, scratch=(), flops=0, name=None, space=pltpu.VMEM, light=False, grant=8):
    size = 0 if light else sum(a.size * a.dtype.itemsize for a in args)
    return pl.pallas_call(
        kernel,
        out_shape=out_shape,
        in_specs=[pl.BlockSpec(memory_space=space)] * len(args),
        out_specs=jax.tree.map(lambda _: pl.BlockSpec(memory_space=pltpu.VMEM), out_shape),
        scratch_shapes=list(scratch),
        compiler_params=pltpu.CompilerParams(vmem_limit_bytes=grant * 1024 * 1024),
        cost_estimate=pl.CostEstimate(flops=int(flops * 6 * N**3), bytes_accessed=size, transcendentals=0),
        name=name,
    )(*args)


def shape(dims, dtype=F32):
    return jax.ShapeDtypeStruct(dims, dtype)


def band_kernel(*refs):
    sources, (band, offset), places, arrived = refs[:5], refs[5:7], refs[7:12], refs[12]
    copies = [pltpu.make_async_copy(a, b, arrived.at[i]) for i, (a, b) in enumerate(zip(sources, places))]
    for copy in copies:
        copy.start()
    for copy in copies:
        copy.wait()
    cond_cov, pred_mean, correction, spread, observed = places
    _, _, _, _, p = place()
    block = lax.broadcasted_iota(jnp.int32, (2, BAND), 1) // 8
    seen = jnp.zeros((2, BAND), F32)
    for i in range(4):
        seen = seen + jnp.where(block == i, observed[:, i : i + 1].astype(F32), 0.0)
    value = pred_mean[...] + seen * correction[...]
    missing = (1.0 - seen) * spread[...]
    offset[...] = value
    lane = lax.broadcasted_iota(jnp.int32, (BAND, N), 1) - p * BAND
    diagonal = lane == lax.broadcasted_iota(jnp.int32, (BAND, N), 0)
    own = jnp.logical_and(lane[:8] >= 0, lane[:8] < BAND)
    wide = jnp.concatenate([jnp.concatenate([part] * 16, axis=1) for part in (missing, value)], axis=0)
    band[0:BAND, :] = cond_cov[0] + jnp.where(diagonal, wide[0:1, :], 0.0)
    band[BAND : 2 * BAND, :] = cond_cov[1] + jnp.where(diagonal, wide[1:2, :], 0.0)
    rows = jnp.concatenate([wide[2:4, :], jnp.zeros((6, N), F32)], axis=0)
    band[2 * BAND :, :] = jnp.where(own, rows, 0.0)


def z_pieces(pieces, rows):
    chip, r1, s1, r2, s2, r3, s3, r4, s4 = pieces
    _, _, z, core, _ = place()
    way = 2 * core - 1
    band = lambda away, c: 2 * lax.rem(z + away + Z, Z) + c
    found = [(chip, 0, band(0, core)), (chip, rows, band(0, 1 - core))]
    for i, (r, s) in enumerate(((r1, s1), (r2, s2), (r3, s3)), 1):
        found += [(r, 0, band(way * i, core)), (r, rows, band(way * i, 1 - core))]
        found += [(s, 0, band(-way * i, 1 - core)), (s, rows, band(-way * i, core))]
    return found + [(r4, 0, band(4, core)), (s4, 0, band(4, 1 - core))]


def half_pieces(pieces, at, lead, height):
    r1, s1, r2, s2 = pieces
    _, _, _, core, _ = place()
    way = 2 * core - 1
    near, far = pl.multiple_of(core * height, height), pl.multiple_of((1 - core) * height, height)
    one, two, three_ = lax.rem(at + way + 4, 4), lax.rem(at - way + 4, 4), lax.rem(at + 2, 4)
    return [
        (r1, lead, one, near),
        (r1, lead + height, one, far),
        (s1, lead, two, far),
        (s1, lead + height, two, near),
        (r2, lead, three_, near),
        (s2, lead, three_, far),
    ]


def store_rolled(dest, lead, whole, core, height):
    near, far = pl.multiple_of(core * height, height), pl.multiple_of((1 - core) * height, height)
    dest[lead : lead + height, :] = whole[pl.ds(near, height), :]
    dest[lead + height : lead + 2 * height, :] = whole[pl.ds(far, height), :]


def triangle():
    return (
        lax.broadcasted_iota(jnp.int32, (HALF, HALF), 0) - lax.broadcasted_iota(jnp.int32, (HALF, HALF), 1)
    )


def pack(dest, cov, vec, scratch, core):
    below = triangle()
    last = cov[HALF:, HALF:]
    scratch[:, :HALF] = cov[:HALF, HALF:]
    scratch[:, HALF:] = jnp.where(below >= 0, cov[:HALF, :HALF], last)
    dest[0:1, :] = vec
    dest[1:2, :HALF] = jnp.sum(jnp.where(below == 0, last, 0.0), axis=0, keepdims=True)
    dest[1:2, HALF:] = jnp.zeros((1, HALF), F32)
    dest[2:8, :] = jnp.zeros((6, N), F32)
    store_rolled(dest, 8, scratch, core, HALF // 2)


def unpack(packed, heads, at, store):
    below = triangle()
    side, mixed = packed[at, :, :HALF], packed[at, :, HALF:]
    turned = mixed.T
    store(0, 0, jnp.where(below >= 0, mixed, turned))
    store(0, HALF, side)
    store(HALF, 0, side.T)
    store(HALF, HALF, jnp.where(below < 0, mixed, jnp.where(below == 0, heads[at, 1:2, :HALF], turned)))


def compose_gain_kernel(*refs):
    pieces, (a0h, a0l, a1h, a1l, bh, bl, sent, b) = refs[:9], refs[9:]
    _, _, _, core, _ = place()
    kept = jnp.where(lax.axis_index("tm") == 15, 0.0, 1.0)
    for source, first, band in z_pieces(pieces, 2 * BAND):
        row = pl.multiple_of(band * BAND, BAND)
        a0h[pl.ds(row, BAND), :], a0l[pl.ds(row, BAND), :] = split(source[first : first + BAND, :])
        a1h[pl.ds(row, BAND), :], a1l[pl.ds(row, BAND), :] = split(
            source[first + BAND : first + 2 * BAND, :] * kept
        )
    b[...] = nn((a0h[...], a0l[...]), (a1h[...], a1l[...]))
    bh[...], bl[...] = split(b[...])
    store_rolled(sent, 0, b, core, HALF)


def congruence(left, state, add, add_vec):
    moved = nt(split(state[...]), left)
    state[:N, :] = nn(left, split(moved[:N])) + add
    state[N:, :] = moved[N:] + add_vec


def compose_cov_kernel(*refs):
    pieces, (a0h, a0l, offset), (cov_bands, offsets, sent, state, cov0, scratch) = refs[:9], refs[9:12], refs[12:]
    _, _, _, core, p = place()
    pads = jnp.zeros((8, N), F32)
    for source, first, band in z_pieces(pieces, 2 * BAND + 8):
        row = pl.multiple_of(band * BAND, BAND)
        cov0[pl.ds(row, BAND), :] = source[first : first + BAND, :]
        state[pl.ds(row, BAND), :] = source[first + BAND : first + 2 * BAND, :]
        pads = pads + source[first + 2 * BAND : first + 2 * BAND + 8, :]
    state[N:, :] = jnp.broadcast_to(pads[1:2], (16, N))
    row = pl.multiple_of(p * BAND, BAND)
    cov_bands[BAND:, :] = state[pl.ds(row, BAND), :]
    moved = nt(split(state[N:, :]), (a0h[pl.ds(row, BAND), :], a0l[pl.ds(row, BAND), :]))
    offsets[0:1, :] = moved[0:1] + offset[0:1, :]
    offsets[1:2, :] = offset[1:2, :]
    congruence((a0h[...], a0l[...]), state, cov0[...], jnp.broadcast_to(pads[0:1], (16, N)))
    cov_bands[:BAND, :] = state[pl.ds(row, BAND), :]
    pack(sent, state[:N, :], state[N : N + 1, :], scratch, core)


def row_gain_kernel(ownh, ownl, r1, s1, r2, s2, s3, bh, bl, sent, ph, plo, total):
    _, x, _, core, _ = place()
    bh[x], bl[x] = ownh[...], ownl[...]
    for source, first, at, row in half_pieces((r1, s1, r2, s2), x, 0, HALF):
        height = source.shape[0] if source is s2 else HALF
        bh[at, pl.ds(row, height), :], bl[at, pl.ds(row, height), :] = split(source[first : first + height, :])
    row = pl.multiple_of((1 - core) * HALF + HALF // 2, HALF // 2)
    at = lax.rem(x + 2, X)
    bh[at, pl.ds(row, HALF // 2), :], bl[at, pl.ds(row, HALF // 2), :] = split(s3[...])
    gain = (bh[3], bl[3])

    def keep(k, value):
        @pl.when(x == k)
        def _():
            ph[...], plo[...] = value

    keep(3, gain)
    keep(2, gain)
    gain = split(nn((bh[2], bl[2]), gain))
    keep(1, gain)
    gain = split(nn((bh[1], bl[1]), gain))
    keep(0, gain)
    total[...] = nn((bh[0], bl[0]), gain)
    store_rolled(sent, 0, total, core, HALF)


def row_cov_kernel(
    own, r1, s1, r2, s2, bh, bl, sent, suffix, suffix_vec, packed, heads, cov, state, scratch
):
    _, x, _, core, _ = place()
    near, far = (pl.multiple_of(c * HALF // 2, HALF // 2) for c in (core, 1 - core))
    own_halves = [(own, 8, x, near), (own, 8 + HALF // 2, x, far)]
    for source, first, at, row in own_halves + half_pieces((r1, s1, r2, s2), x, 8, HALF // 2):
        packed[at, pl.ds(row, HALF // 2), :] = source[first : first + HALF // 2, :]
        heads[at] = source[0:8, :]
    vecs = lambda k: jnp.broadcast_to(heads[k, 0:1, :], (16, N))

    def into(dest):
        def store(row, column, value):
            dest[row : row + HALF, column : column + HALF] = value

        return store

    unpack(packed, heads, 3, into(state))
    state[N:, :] = vecs(3)

    @pl.when(x >= 2)
    def _():
        suffix[...], suffix_vec[...] = state[:N, :], state[N : N + 8, :]

    for k in (2, 1, 0):
        unpack(packed, heads, k, into(cov))
        congruence((bh[k], bl[k]), state, cov[...], vecs(k))
        if k:

            @pl.when(x == k - 1)
            def _():
                suffix[...], suffix_vec[...] = state[:N, :], state[N : N + 8, :]

    pack(sent, state[:N, :], state[N : N + 1, :], scratch, core)


def mirrored(packed, heads, high, low):
    def store(row, column, value):
        at = (slice(row, row + HALF), slice(column, column + HALF))
        high[at], low[at] = split(value)

    unpack(packed, heads, 0, store)


def mean_of(head, left):
    return few_nt(split(jnp.broadcast_to(head, (16, N))), left)


def own_kernel(a1h, a1l, bh, bl, ph, plo, suffix, suffix_vec, vh, vl, base, mean):
    _, x, _, _, p = place()
    row = pl.multiple_of(p * BAND, BAND)
    band = tuple(
        jnp.concatenate([one[pl.ds(row, BAND), :], zero[pl.ds(row, BAND), :]], axis=0)
        for one, zero in ((a1h, bh), (a1l, bl))
    )
    vh[...], vl[...] = band
    base[...] = jnp.zeros_like(base)
    mean[...] = jnp.zeros_like(mean)

    @pl.when(x < X - 1)
    def _():
        base[...] = few_nn(band, split(suffix[...]))
        mean[...] = mean_of(suffix_vec[0:1, :], band)
        vh[...], vl[...] = split(few_nn(band, (ph[...], plo[...])))


def above_kernel(t1, ts, vh, vl, th, tl, wh, wl):
    y, _, _, core, _ = place()
    for mine, source in ((0, ts), (1, t1)):

        @pl.when(jnp.logical_and(core == mine, y < 2))
        def _():
            th[HALF:, :], tl[HALF:, :] = split(source[:HALF, :])
            th[:HALF, :], tl[:HALF, :] = split(source[HALF:, :])
            wh[...], wl[...] = split(few_nn((vh[...], vl[...]), (th[...], tl[...])))


def near_kernel(d1, ds, vh, vl, mean_in, belowh, belowl, below_vec, near, mean, packed, heads, dh, dl):
    y, _, _, core, _ = place()
    near[...] = jnp.zeros_like(near)
    mean[...] = mean_in[...]
    quarter = HALF // 2

    def take(source, first):
        packed[0, first * quarter : (first + 1) * quarter, :] = source[8 : 8 + quarter, :]
        packed[0, (1 - first) * quarter : (2 - first) * quarter, :] = source[8 + quarter :, :]
        heads[0] = source[0:8, :]

    for mine, above, below in ((0, ds, d1), (1, d1, ds)):

        @pl.when(jnp.logical_and(core == mine, y < 3))
        def _():
            take(above, 1)
            mirrored(packed, heads, dh, dl)
            near[...] = few_nn((vh[...], vl[...]), (dh[...], dl[...]))
            mean[...] += mean_of(heads[0, 0:1, :], (vh[...], vl[...]))

        @pl.when(jnp.logical_and(core == mine, y == 0))
        def _():
            take(below, 0)
            mirrored(packed, heads, belowh, belowl)
            below_vec[...] = heads[0]


def middle_kernel(t2, ts, wh, wl, belowh, belowl, below_vec, mean, beyond, mean_out, th, tl):
    y, _, _, core, _ = place()
    beyond[...] = jnp.zeros_like(beyond)
    mean_out[...] = mean[...]

    @pl.when(y == 0)
    def _():
        mine, its = (pl.multiple_of(c * HALF, HALF) for c in (core, 1 - core))
        th[pl.ds(mine, HALF), :], tl[pl.ds(mine, HALF), :] = split(t2[...])
        th[pl.ds(its, HALF), :], tl[pl.ds(its, HALF), :] = split(ts[...])
        far = (th[...], tl[...])
        left = split(few_nn((wh[...], wl[...]), far))
        mean_out[...] += mean_of(below_vec[0:1, :], left)
        beyond[...] = few_nt(split(few_nn(left, (belowh[...], belowl[...]))), far)


def last_kernel(
    d2, ds, beyond, near, base, mean_in, wh, wl, th, tl, ph, plo, a1h, a1l, bh, bl, cov_bands, offsets,
    mean, out, packed, heads, dh, dl, moved, row_mean,
):
    y, x, _, core, _ = place()
    moved[...] = near[...]
    row_mean[...] = mean_in[...]

    @pl.when(y < 2)
    def _():
        quarter = HALF // 2
        packed[0, pl.ds(pl.multiple_of(core * quarter, quarter), quarter), :] = d2[8:, :]
        packed[0, pl.ds(pl.multiple_of((1 - core) * quarter, quarter), quarter), :] = ds[8:, :]
        heads[0] = d2[0:8, :]
        mirrored(packed, heads, dh, dl)
        left = (wh[...], wl[...])
        row_mean[...] += mean_of(heads[0, 0:1, :], left)
        past = few_nn(left, (dh[...], dl[...])) + beyond[...]
        moved[...] += few_nt(split(past), (th[...], tl[...]))

    @pl.when(x < X - 1)
    def _():
        moved[...] = few_nt(split(moved[...]), (ph[...], plo[...])) + base[...]

    out[1] = few_nt(split(moved[:BAND, :]), (a1h[...], a1l[...])) + cov_bands[BAND:, :]
    out[0] = few_nt(split(moved[BAND:, :]), (bh[...], bl[...])) + cov_bands[:BAND, :]
    mean[1:2, :] = row_mean[0:1, :BAND] + offsets[1:2, :]
    mean[0:1, :] = row_mean[0:1, BAND : 2 * BAND] + offsets[0:1, :]


def device(y, x, z, core):
    return ((y % Y) * X + x % X) * 16 + (z % Z) * 2 + core


def perm(dy, dx, dz):
    return [
        (device(y, x, z, c), device(y + (1 - 2 * c) * dy, x + (1 - 2 * c) * dx, z + (1 - 2 * c) * dz, c))
        for y in range(Y)
        for x in range(X)
        for z in range(Z)
        for c in range(2)
    ]


AXES = ("tm", "panel")
ROUND_Y, ROUND_X, ROUND_Z, TWO_Z = perm(1, 0, 0), perm(0, 1, 0), perm(0, 0, 1), perm(0, 0, 2)
SWAP = [(i, i ^ 1) for i in range(256)]


def swap(piece):
    return lax.ppermute(piece, AXES, SWAP)


def gather_z(first, second):
    rows, now = first.rows, first.now
    r1 = hop(now, ROUND_Z)
    r2, r3 = hop(r1, ROUND_Z), hop(r1, TWO_Z)
    r4 = hop(r2[:rows], TWO_Z)
    for _ in range(4):
        second.go()
    return [now, r1, swap(r1), r2, swap(r2), r3, swap(r3), r4, swap(r4)], second.finish()


class Turn:
    def __init__(self, own):
        self.rows, self.hop, self.pieces = own.shape[0], 0, []
        self.near = swap(own)
        self.now = jnp.concatenate([own, self.near], axis=0)

    def go(self):
        self.pieces += [self.now, swap(self.now)] if self.hop else [self.now]
        self.hop += 1
        self.now = hop(self.now if self.hop < 4 else self.now[: self.rows], ROUND_Z)

    def finish(self):
        return [*self.pieces, self.now, swap(self.now)]


def together(*values):
    return lax.optimization_barrier(values)


def after(value, *others):
    return together(value, *others)[0]


def hop(sent, way):
    return lax.ppermute(sent, AXES, way)


def first_half(sent):
    return sent[: (sent.shape[0] + 8) // 16 * 8]


def shards(gain, cond_cov, pred_mean, correction, spread, observed):
    square, row8, half = shape((N, N)), shape((8, N)), shape((N, N), BF16)
    first = Turn(gain.reshape(2 * BAND, N))
    args = (cond_cov, pred_mean, correction, spread[None, :], observed)
    band, offset = call(
        band_kernel,
        (shape((2 * BAND + 8, N)), shape((2, BAND))),
        args,
        (*[pltpu.VMEM(a.shape, a.dtype) for a in args[:5]], pltpu.SemaphoreType.DMA((5,))),
        name="band",
        space=pltpu.HBM,
        grant=60,
    )
    a_pieces, c_pieces = gather_z(first, Turn(band))
    a0h, a0l, a1h, a1l, b0h, b0l, sent = call(
        compose_gain_kernel,
        (half, half, half, half, half, half, square),
        a_pieces,
        (pltpu.VMEM((N, N), F32),),
        flops=1,
        name="compose_gain",
    )
    b1 = hop(sent, ROUND_X)
    state = pltpu.VMEM((N + 16, N), F32)
    scratch = pltpu.VMEM((HALF, N), F32)
    packed_four = (pltpu.VMEM((4, HALF, N), F32), pltpu.VMEM((4, 8, N), F32))
    cov_bands, offsets, c0 = call(
        compose_cov_kernel,
        (shape((2 * BAND, N)), shape((2, BAND)), shape((HALF + 8, N))),
        (*c_pieces, a0h, a0l, offset),
        (state, pltpu.VMEM((N, N), F32), scratch),
        flops=9,
        name="compose_cov",
    )
    c1 = hop(c0, ROUND_X)
    b2, c2 = hop(first_half(after(b1, offsets)), ROUND_X), hop(first_half(c1), ROUND_X)
    c_near, c_far = swap(c1), swap(c2)
    b_pieces, c_pieces = (b1, swap(b1), b2, after(swap(b2[:128]), c_near), swap(b2[128:])), (c1, c_near, c2, c_far)
    four = shape((4, N, N), BF16)
    bh, bl, sent, ph, plo = call(
        row_gain_kernel,
        (four, four, square, half, half),
        (b0h, b0l, *b_pieces),
        (pltpu.VMEM((N, N), F32),),
        name="row_gain",
        light=True,
    )
    t1 = hop(after(sent, c2), ROUND_Y)
    sent, suffix, suffix_vec = call(
        row_cov_kernel,
        (shape((HALF + 8, N)), square, row8),
        (c0, *c_pieces, bh, bl),
        (*packed_four, pltpu.VMEM((N, N), F32), state, scratch),
        flops=6,
        name="row_cov",
    )
    d1 = hop(sent, ROUND_Y)
    rows, vecs = shape((2 * BAND, N), BF16), shape((16, 2 * BAND))
    plain = shape((2 * BAND, N))
    one_packed = (pltpu.VMEM((1, HALF, N), F32), pltpu.VMEM((1, 8, N), F32))
    whole = (pltpu.VMEM((N, N), BF16), pltpu.VMEM((N, N), BF16))
    vh, vl, base, mean = call(
        own_kernel,
        (rows, rows, plain, vecs),
        (a1h, a1l, b0h, b0l, ph, plo, suffix, suffix_vec),
        flops=1,
        name="own",
    )
    t2 = hop(first_half(after(t1, mean)), ROUND_Y)
    t_near, d_near = swap(after(t1, base)), swap(d1)
    th, tl, wh, wl = call(
        above_kernel, (half, half, rows, rows), (t1, t_near, vh, vl), flops=1, name="above"
    )
    d2 = hop(first_half(d1), ROUND_Y)
    belowh, belowl, below_vec, near, mean = call(
        near_kernel,
        (half, half, row8, plain, vecs),
        (d1, d_near, vh, vl, mean),
        (*one_packed, *whole),
        flops=1,
        name="near",
    )
    t_far, d_far = swap(after(t2, d2)), swap(d2)
    beyond, mean = call(
        middle_kernel,
        (plain, vecs),
        (t2, t_far, wh, wl, belowh, belowl, below_vec, mean),
        whole,
        flops=2,
        name="middle",
    )
    return call(
        last_kernel,
        (shape((2, BAND)), shape((2, BAND, N))),
        (d2, d_far, beyond, near, base, mean, wh, wl, th, tl, ph, plo, a1h, a1l, b0h, b0l, cov_bands, offsets),
        (*one_packed, *whole, pltpu.VMEM((2 * BAND, N), F32), pltpu.VMEM((16, 2 * BAND), F32)),
        flops=1,
        name="last",
    )


def solution(mesh):
    placed = (
        P("tm", "panel", None),
        P("tm", "panel", None),
        P("tm", "panel"),
        P("tm", "panel"),
        P("panel"),
        P("tm", "panel"),
    )
    return jax.shard_map(
        shards,
        mesh=mesh,
        in_specs=placed,
        out_specs=(P("tm", "panel"), P("tm", "panel", None)),
        check_vma=False,
    )
```

```python
import functools
import jax
import jax.numpy as jnp
from jax import lax
from jax.experimental import pallas as pl
from jax.experimental.pallas import tpu as pltpu
from jax.sharding import PartitionSpec as P

F32 = jnp.float32
BF16 = jnp.bfloat16
N = 512
HALF = 256
BAND = 32
X = 4
Y = 4
Z = 8


def split(value):
    high = value.astype(BF16)
    return high, (value - high.astype(F32)).astype(BF16)


def dot(left, right, dims):
    return lax.dot_general(left, right, (dims, ((), ())), preferred_element_type=F32)


def three(left, right, dims):
    (lh, ll), (rh, rl) = left, right
    return dot(lh, rh, dims) + (dot(lh, rl, dims) + dot(ll, rh, dims))


def few(left, right, dims):
    (lh, ll), (rh, rl) = left, right
    rows = lh.shape[0]
    both = dot(jnp.concatenate([lh, ll], axis=0), rh, dims)
    return both[:rows] + (both[rows:] + dot(lh, rl, dims))


def few_nn(left, right):
    return few(left, right, ((1,), (0,)))


def few_nt(left, right):
    return few(left, right, ((1,), (1,)))


def nn(left, right):
    return three(left, right, ((1,), (0,)))


def nt(left, right):
    return three(left, right, ((1,), (1,)))


def place():
    t, p = lax.axis_index("tm"), lax.axis_index("panel")
    return t // X, lax.rem(t, X), p // 2, lax.rem(p, 2), p


def call(kernel, out_shape, args, scratch=(), flops=0, name=None, space=pltpu.VMEM, light=False, grant=8):
    size = 0 if light else sum(a.size * a.dtype.itemsize for a in args)
    return pl.pallas_call(
        kernel,
        out_shape=out_shape,
        in_specs=[pl.BlockSpec(memory_space=space)] * len(args),
        out_specs=jax.tree.map(lambda _: pl.BlockSpec(memory_space=pltpu.VMEM), out_shape),
        scratch_shapes=list(scratch),
        compiler_params=pltpu.CompilerParams(vmem_limit_bytes=grant * 1024 * 1024),
        cost_estimate=pl.CostEstimate(flops=int(flops * 6 * N**3), bytes_accessed=size, transcendentals=0),
        name=name,
    )(*args)


def shape(dims, dtype=F32):
    return jax.ShapeDtypeStruct(dims, dtype)


def band_kernel(*refs):
    sources, (band, offset), places, arrived = refs[:5], refs[5:7], refs[7:12], refs[12]
    copies = [pltpu.make_async_copy(a, b, arrived.at[i]) for i, (a, b) in enumerate(zip(sources, places))]
    for copy in copies:
        copy.start()
    for copy in copies:
        copy.wait()
    cond_cov, pred_mean, correction, spread, observed = places
    _, _, _, _, p = place()
    block = lax.broadcasted_iota(jnp.int32, (2, BAND), 1) // 8
    seen = jnp.zeros((2, BAND), F32)
    for i in range(4):
        seen = seen + jnp.where(block == i, observed[:, i : i + 1].astype(F32), 0.0)
    value = pred_mean[...] + seen * correction[...]
    missing = (1.0 - seen) * spread[...]
    offset[...] = value
    lane = lax.broadcasted_iota(jnp.int32, (BAND, N), 1) - p * BAND
    diagonal = lane == lax.broadcasted_iota(jnp.int32, (BAND, N), 0)
    own = jnp.logical_and(lane[:8] >= 0, lane[:8] < BAND)
    wide = jnp.concatenate([jnp.concatenate([part] * 16, axis=1) for part in (missing, value)], axis=0)
    band[0:BAND, :] = cond_cov[0] + jnp.where(diagonal, wide[0:1, :], 0.0)
    band[BAND : 2 * BAND, :] = cond_cov[1] + jnp.where(diagonal, wide[1:2, :], 0.0)
    rows = jnp.concatenate([wide[2:4, :], jnp.zeros((6, N), F32)], axis=0)
    band[2 * BAND :, :] = jnp.where(own, rows, 0.0)


def z_pieces(pieces, rows):
    chip, r1, s1, r2, s2, r3, s3, r4, s4 = pieces
    _, _, z, core, _ = place()
    way = 2 * core - 1
    band = lambda away, c: 2 * lax.rem(z + away + Z, Z) + c
    found = [(chip, 0, band(0, core)), (chip, rows, band(0, 1 - core))]
    for i, (r, s) in enumerate(((r1, s1), (r2, s2), (r3, s3)), 1):
        found += [(r, 0, band(way * i, core)), (r, rows, band(way * i, 1 - core))]
        found += [(s, 0, band(-way * i, 1 - core)), (s, rows, band(-way * i, core))]
    return found + [(r4, 0, band(4, core)), (s4, 0, band(4, 1 - core))]


def half_pieces(pieces, at, lead, height):
    r1, s1, r2, s2 = pieces
    _, _, _, core, _ = place()
    way = 2 * core - 1
    near, far = pl.multiple_of(core * height, height), pl.multiple_of((1 - core) * height, height)
    one, two, three_ = lax.rem(at + way + 4, 4), lax.rem(at - way + 4, 4), lax.rem(at + 2, 4)
    return [
        (r1, lead, one, near),
        (r1, lead + height, one, far),
        (s1, lead, two, far),
        (s1, lead + height, two, near),
        (r2, lead, three_, near),
        (s2, lead, three_, far),
    ]


def store_rolled(dest, lead, whole, core, height):
    near, far = pl.multiple_of(core * height, height), pl.multiple_of((1 - core) * height, height)
    dest[lead : lead + height, :] = whole[pl.ds(near, height), :]
    dest[lead + height : lead + 2 * height, :] = whole[pl.ds(far, height), :]


def triangle():
    return (
        lax.broadcasted_iota(jnp.int32, (HALF, HALF), 0) - lax.broadcasted_iota(jnp.int32, (HALF, HALF), 1)
    )


def pack(dest, cov, vec, scratch, core):
    below = triangle()
    last = cov[HALF:, HALF:]
    scratch[:, :HALF] = cov[:HALF, HALF:]
    scratch[:, HALF:] = jnp.where(below >= 0, cov[:HALF, :HALF], last)
    dest[0:1, :] = vec
    dest[1:2, :HALF] = jnp.sum(jnp.where(below == 0, last, 0.0), axis=0, keepdims=True)
    dest[1:2, HALF:] = jnp.zeros((1, HALF), F32)
    dest[2:8, :] = jnp.zeros((6, N), F32)
    store_rolled(dest, 8, scratch, core, HALF // 2)


def unpack(packed, heads, at, store):
    below = triangle()
    side, mixed = packed[at, :, :HALF], packed[at, :, HALF:]
    turned = mixed.T
    store(0, 0, jnp.where(below >= 0, mixed, turned))
    store(0, HALF, side)
    store(HALF, 0, side.T)
    store(HALF, HALF, jnp.where(below < 0, mixed, jnp.where(below == 0, heads[at, 1:2, :HALF], turned)))


def compose_gain_kernel(*refs):
    pieces, (a0h, a0l, a1h, a1l, bh, bl, sent, b) = refs[:9], refs[9:]
    _, _, _, core, _ = place()
    kept = jnp.where(lax.axis_index("tm") == 15, 0.0, 1.0)
    for source, first, band in z_pieces(pieces, 2 * BAND):
        row = pl.multiple_of(band * BAND, BAND)
        a0h[pl.ds(row, BAND), :], a0l[pl.ds(row, BAND), :] = split(source[first : first + BAND, :])
        a1h[pl.ds(row, BAND), :], a1l[pl.ds(row, BAND), :] = split(
            source[first + BAND : first + 2 * BAND, :] * kept
        )
    b[...] = nn((a0h[...], a0l[...]), (a1h[...], a1l[...]))
    bh[...], bl[...] = split(b[...])
    store_rolled(sent, 0, b, core, HALF)


def congruence(left, state, add, add_vec):
    moved = nt(split(state[...]), left)
    state[:N, :] = nn(left, split(moved[:N])) + add
    state[N:, :] = moved[N:] + add_vec


def compose_cov_kernel(*refs):
    pieces, (a0h, a0l, offset), (cov_bands, offsets, sent, state, cov0, scratch) = refs[:9], refs[9:12], refs[12:]
    _, _, _, core, p = place()
    pads = jnp.zeros((8, N), F32)
    for source, first, band in z_pieces(pieces, 2 * BAND + 8):
        row = pl.multiple_of(band * BAND, BAND)
        cov0[pl.ds(row, BAND), :] = source[first : first + BAND, :]
        state[pl.ds(row, BAND), :] = source[first + BAND : first + 2 * BAND, :]
        pads = pads + source[first + 2 * BAND : first + 2 * BAND + 8, :]
    state[N:, :] = jnp.broadcast_to(pads[1:2], (16, N))
    row = pl.multiple_of(p * BAND, BAND)
    cov_bands[BAND:, :] = state[pl.ds(row, BAND), :]
    moved = nt(split(state[N:, :]), (a0h[pl.ds(row, BAND), :], a0l[pl.ds(row, BAND), :]))
    offsets[0:1, :] = moved[0:1] + offset[0:1, :]
    offsets[1:2, :] = offset[1:2, :]
    congruence((a0h[...], a0l[...]), state, cov0[...], jnp.broadcast_to(pads[0:1], (16, N)))
    cov_bands[:BAND, :] = state[pl.ds(row, BAND), :]
    pack(sent, state[:N, :], state[N : N + 1, :], scratch, core)


def row_gain_kernel(ownh, ownl, r1, s1, r2, s2, s3, bh, bl, sent, ph, plo, total):
    _, x, _, core, _ = place()
    bh[x], bl[x] = ownh[...], ownl[...]
    for source, first, at, row in half_pieces((r1, s1, r2, s2), x, 0, HALF):
        height = source.shape[0] if source is s2 else HALF
        bh[at, pl.ds(row, height), :], bl[at, pl.ds(row, height), :] = split(source[first : first + height, :])
    row = pl.multiple_of((1 - core) * HALF + HALF // 2, HALF // 2)
    at = lax.rem(x + 2, X)
    bh[at, pl.ds(row, HALF // 2), :], bl[at, pl.ds(row, HALF // 2), :] = split(s3[...])
    gain = (bh[3], bl[3])

    def keep(k, value):
        @pl.when(x == k)
        def _():
            ph[...], plo[...] = value

    keep(3, gain)
    keep(2, gain)
    gain = split(nn((bh[2], bl[2]), gain))
    keep(1, gain)
    gain = split(nn((bh[1], bl[1]), gain))
    keep(0, gain)
    total[...] = nn((bh[0], bl[0]), gain)
    store_rolled(sent, 0, total, core, HALF)


def row_cov_kernel(
    own, r1, s1, r2, s2, bh, bl, sent, suffix, suffix_vec, packed, heads, cov, state, scratch
):
    _, x, _, core, _ = place()
    near, far = (pl.multiple_of(c * HALF // 2, HALF // 2) for c in (core, 1 - core))
    own_halves = [(own, 8, x, near), (own, 8 + HALF // 2, x, far)]
    for source, first, at, row in own_halves + half_pieces((r1, s1, r2, s2), x, 8, HALF // 2):
        packed[at, pl.ds(row, HALF // 2), :] = source[first : first + HALF // 2, :]
        heads[at] = source[0:8, :]
    vecs = lambda k: jnp.broadcast_to(heads[k, 0:1, :], (16, N))

    def into(dest):
        def store(row, column, value):
            dest[row : row + HALF, column : column + HALF] = value

        return store

    unpack(packed, heads, 3, into(state))
    state[N:, :] = vecs(3)

    @pl.when(x >= 2)
    def _():
        suffix[...], suffix_vec[...] = state[:N, :], state[N : N + 8, :]

    for k in (2, 1, 0):
        unpack(packed, heads, k, into(cov))
        congruence((bh[k], bl[k]), state, cov[...], vecs(k))
        if k:

            @pl.when(x == k - 1)
            def _():
                suffix[...], suffix_vec[...] = state[:N, :], state[N : N + 8, :]

    pack(sent, state[:N, :], state[N : N + 1, :], scratch, core)


def mirrored(packed, heads, high, low):
    def store(row, column, value):
        at = (slice(row, row + HALF), slice(column, column + HALF))
        high[at], low[at] = split(value)

    unpack(packed, heads, 0, store)


def mean_of(head, left):
    return few_nt(split(jnp.broadcast_to(head, (16, N))), left)


def own_kernel(a1h, a1l, bh, bl, ph, plo, suffix, suffix_vec, vh, vl, base, mean):
    _, x, _, _, p = place()
    row = pl.multiple_of(p * BAND, BAND)
    band = tuple(
        jnp.concatenate([one[pl.ds(row, BAND), :], zero[pl.ds(row, BAND), :]], axis=0)
        for one, zero in ((a1h, bh), (a1l, bl))
    )
    vh[...], vl[...] = band
    base[...] = jnp.zeros_like(base)
    mean[...] = jnp.zeros_like(mean)

    @pl.when(x < X - 1)
    def _():
        base[...] = few_nn(band, split(suffix[...]))
        mean[...] = mean_of(suffix_vec[0:1, :], band)
        vh[...], vl[...] = split(few_nn(band, (ph[...], plo[...])))


def above_kernel(t1, ts, vh, vl, th, tl, wh, wl):
    y, _, _, core, _ = place()
    for mine, source in ((0, ts), (1, t1)):

        @pl.when(jnp.logical_and(core == mine, y < 2))
        def _():
            th[HALF:, :], tl[HALF:, :] = split(source[:HALF, :])
            th[:HALF, :], tl[:HALF, :] = split(source[HALF:, :])
            wh[...], wl[...] = split(few_nn((vh[...], vl[...]), (th[...], tl[...])))


def near_kernel(d1, ds, vh, vl, mean_in, belowh, belowl, below_vec, near, mean, packed, heads, dh, dl):
    y, _, _, core, _ = place()
    near[...] = jnp.zeros_like(near)
    mean[...] = mean_in[...]
    quarter = HALF // 2

    def take(source, first):
        packed[0, first * quarter : (first + 1) * quarter, :] = source[8 : 8 + quarter, :]
        packed[0, (1 - first) * quarter : (2 - first) * quarter, :] = source[8 + quarter :, :]
        heads[0] = source[0:8, :]

    for mine, above, below in ((0, ds, d1), (1, d1, ds)):

        @pl.when(jnp.logical_and(core == mine, y < 3))
        def _():
            take(above, 1)
            mirrored(packed, heads, dh, dl)
            near[...] = few_nn((vh[...], vl[...]), (dh[...], dl[...]))
            mean[...] += mean_of(heads[0, 0:1, :], (vh[...], vl[...]))

        @pl.when(jnp.logical_and(core == mine, y == 0))
        def _():
            take(below, 0)
            mirrored(packed, heads, belowh, belowl)
            below_vec[...] = heads[0]


def middle_kernel(t2, ts, wh, wl, belowh, belowl, below_vec, mean, beyond, mean_out, th, tl):
    y, _, _, core, _ = place()
    beyond[...] = jnp.zeros_like(beyond)
    mean_out[...] = mean[...]

    @pl.when(y == 0)
    def _():
        mine, its = (pl.multiple_of(c * HALF, HALF) for c in (core, 1 - core))
        th[pl.ds(mine, HALF), :], tl[pl.ds(mine, HALF), :] = split(t2[...])
        th[pl.ds(its, HALF), :], tl[pl.ds(its, HALF), :] = split(ts[...])
        far = (th[...], tl[...])
        left = split(few_nn((wh[...], wl[...]), far))
        mean_out[...] += mean_of(below_vec[0:1, :], left)
        beyond[...] = few_nt(split(few_nn(left, (belowh[...], belowl[...]))), far)


def last_kernel(
    d2, ds, beyond, near, base, mean_in, wh, wl, th, tl, ph, plo, a1h, a1l, bh, bl, cov_bands, offsets,
    mean, out, packed, heads, dh, dl, moved, row_mean,
):
    y, x, _, core, _ = place()
    moved[...] = near[...]
    row_mean[...] = mean_in[...]

    @pl.when(y < 2)
    def _():
        quarter = HALF // 2
        packed[0, pl.ds(pl.multiple_of(core * quarter, quarter), quarter), :] = d2[8:, :]
        packed[0, pl.ds(pl.multiple_of((1 - core) * quarter, quarter), quarter), :] = ds[8:, :]
        heads[0] = d2[0:8, :]
        mirrored(packed, heads, dh, dl)
        left = (wh[...], wl[...])
        row_mean[...] += mean_of(heads[0, 0:1, :], left)
        past = few_nn(left, (dh[...], dl[...])) + beyond[...]
        moved[...] += few_nt(split(past), (th[...], tl[...]))

    @pl.when(x < X - 1)
    def _():
        moved[...] = few_nt(split(moved[...]), (ph[...], plo[...])) + base[...]

    out[1] = few_nt(split(moved[:BAND, :]), (a1h[...], a1l[...])) + cov_bands[BAND:, :]
    out[0] = few_nt(split(moved[BAND:, :]), (bh[...], bl[...])) + cov_bands[:BAND, :]
    mean[1:2, :] = row_mean[0:1, :BAND] + offsets[1:2, :]
    mean[0:1, :] = row_mean[0:1, BAND : 2 * BAND] + offsets[0:1, :]


def device(y, x, z, core):
    return ((y % Y) * X + x % X) * 16 + (z % Z) * 2 + core


def perm(dy, dx, dz):
    return [
        (device(y, x, z, c), device(y + (1 - 2 * c) * dy, x + (1 - 2 * c) * dx, z + (1 - 2 * c) * dz, c))
        for y in range(Y)
        for x in range(X)
        for z in range(Z)
        for c in range(2)
    ]


AXES = ("tm", "panel")
ROUND_Y, ROUND_X, ROUND_Z, TWO_Z = perm(1, 0, 0), perm(0, 1, 0), perm(0, 0, 1), perm(0, 0, 2)
SWAP = [(i, i ^ 1) for i in range(256)]


def swap(piece):
    return lax.ppermute(piece, AXES, SWAP)


def gather_z(first, second):
    rows, now = first.rows, first.now
    r1 = hop(now, ROUND_Z)
    r2, r3 = hop(r1, ROUND_Z), hop(r1, TWO_Z)
    r4 = hop(r2[:rows], TWO_Z)
    for _ in range(4):
        second.go()
    return [now, r1, swap(r1), r2, swap(r2), r3, swap(r3), r4, swap(r4)], second.finish()


class Turn:
    def __init__(self, own):
        self.rows, self.hop, self.pieces = own.shape[0], 0, []
        self.near = swap(own)
        below, above = ((0, self.rows, 0), (0, 0, 0)), ((self.rows, 0, 0), (0, 0, 0))
        self.now = lax.pad(own, 0.0, below) + lax.pad(self.near, 0.0, above)

    def go(self):
        self.pieces += [self.now, swap(self.now)] if self.hop else [self.now]
        self.hop += 1
        self.now = hop(self.now if self.hop < 4 else self.now[: self.rows], ROUND_Z)

    def finish(self):
        return [*self.pieces, self.now, swap(self.now)]


def together(*values):
    return lax.optimization_barrier(values)


def after(value, *others):
    return together(value, *others)[0]


def hop(sent, way):
    return lax.ppermute(sent, AXES, way)


def first_half(sent):
    return sent[: (sent.shape[0] + 8) // 16 * 8]


def shards(gain, cond_cov, pred_mean, correction, spread, observed):
    square, row8, half = shape((N, N)), shape((8, N)), shape((N, N), BF16)
    first = Turn(gain.reshape(2 * BAND, N))
    args = (cond_cov, pred_mean, correction, spread[None, :], observed)
    band, offset = call(
        band_kernel,
        (shape((2 * BAND + 8, N)), shape((2, BAND))),
        args,
        (*[pltpu.VMEM(a.shape, a.dtype) for a in args[:5]], pltpu.SemaphoreType.DMA((5,))),
        name="band",
        space=pltpu.HBM,
        grant=60,
    )
    a_pieces, c_pieces = gather_z(first, Turn(band))
    a0h, a0l, a1h, a1l, b0h, b0l, sent = call(
        compose_gain_kernel,
        (half, half, half, half, half, half, square),
        a_pieces,
        (pltpu.VMEM((N, N), F32),),
        flops=1,
        name="compose_gain",
    )
    b1 = hop(sent, ROUND_X)
    state = pltpu.VMEM((N + 16, N), F32)
    scratch = pltpu.VMEM((HALF, N), F32)
    packed_four = (pltpu.VMEM((4, HALF, N), F32), pltpu.VMEM((4, 8, N), F32))
    cov_bands, offsets, c0 = call(
        compose_cov_kernel,
        (shape((2 * BAND, N)), shape((2, BAND)), shape((HALF + 8, N))),
        (*c_pieces, a0h, a0l, offset),
        (state, pltpu.VMEM((N, N), F32), scratch),
        flops=9,
        name="compose_cov",
    )
    c1 = hop(c0, ROUND_X)
    b2, c2 = hop(first_half(after(b1, offsets)), ROUND_X), hop(first_half(c1), ROUND_X)
    c_near, c_far = swap(c1), swap(c2)
    b_pieces, c_pieces = (b1, swap(b1), b2, after(swap(b2[:128]), c_near), swap(b2[128:])), (c1, c_near, c2, c_far)
    four = shape((4, N, N), BF16)
    bh, bl, sent, ph, plo = call(
        row_gain_kernel,
        (four, four, square, half, half),
        (b0h, b0l, *b_pieces),
        (pltpu.VMEM((N, N), F32),),
        name="row_gain",
        light=True,
    )
    t1 = hop(after(sent, c2), ROUND_Y)
    sent, suffix, suffix_vec = call(
        row_cov_kernel,
        (shape((HALF + 8, N)), square, row8),
        (c0, *c_pieces, bh, bl),
        (*packed_four, pltpu.VMEM((N, N), F32), state, scratch),
        flops=6,
        name="row_cov",
    )
    d1 = hop(sent, ROUND_Y)
    rows, vecs = shape((2 * BAND, N), BF16), shape((16, 2 * BAND))
    plain = shape((2 * BAND, N))
    one_packed = (pltpu.VMEM((1, HALF, N), F32), pltpu.VMEM((1, 8, N), F32))
    whole = (pltpu.VMEM((N, N), BF16), pltpu.VMEM((N, N), BF16))
    vh, vl, base, mean = call(
        own_kernel,
        (rows, rows, plain, vecs),
        (a1h, a1l, b0h, b0l, ph, plo, suffix, suffix_vec),
        flops=1,
        name="own",
    )
    t2 = hop(first_half(after(t1, mean)), ROUND_Y)
    t_near, d_near = swap(after(t1, base)), swap(d1)
    th, tl, wh, wl = call(
        above_kernel, (half, half, rows, rows), (t1, t_near, vh, vl), flops=1, name="above"
    )
    d2 = hop(first_half(d1), ROUND_Y)
    belowh, belowl, below_vec, near, mean = call(
        near_kernel,
        (half, half, row8, plain, vecs),
        (d1, d_near, vh, vl, mean),
        (*one_packed, *whole),
        flops=1,
        name="near",
    )
    t_far, d_far = swap(after(t2, d2)), swap(d2)
    beyond, mean = call(
        middle_kernel,
        (plain, vecs),
        (t2, t_far, wh, wl, belowh, belowl, below_vec, mean),
        whole,
        flops=2,
        name="middle",
    )
    return call(
        last_kernel,
        (shape((2, BAND)), shape((2, BAND, N))),
        (d2, d_far, beyond, near, base, mean, wh, wl, th, tl, ph, plo, a1h, a1l, b0h, b0l, cov_bands, offsets),
        (*one_packed, *whole, pltpu.VMEM((2 * BAND, N), F32), pltpu.VMEM((16, 2 * BAND), F32)),
        flops=1,
        name="last",
    )


def solution(mesh):
    placed = (
        P("tm", "panel", None),
        P("tm", "panel", None),
        P("tm", "panel"),
        P("tm", "panel"),
        P("panel"),
        P("tm", "panel"),
    )
    return jax.shard_map(
        shards,
        mesh=mesh,
        in_specs=placed,
        out_specs=(P("tm", "panel"), P("tm", "panel", None)),
        check_vma=False,
    )
```

```python
import functools
import jax
import jax.numpy as jnp
from jax import lax
from jax.experimental import pallas as pl
from jax.experimental.pallas import tpu as pltpu
from jax.sharding import PartitionSpec as P

F32 = jnp.float32
BF16 = jnp.bfloat16
N = 512
HALF = 256
BAND = 32
X = 4
Y = 4
Z = 8


def split(value):
    high = value.astype(BF16)
    return high, (value - high.astype(F32)).astype(BF16)


def dot(left, right, dims):
    return lax.dot_general(left, right, (dims, ((), ())), preferred_element_type=F32)


def three(left, right, dims):
    (lh, ll), (rh, rl) = left, right
    return dot(lh, rh, dims) + (dot(lh, rl, dims) + dot(ll, rh, dims))


def few(left, right, dims):
    (lh, ll), (rh, rl) = left, right
    rows = lh.shape[0]
    both = dot(jnp.concatenate([lh, ll], axis=0), rh, dims)
    return both[:rows] + (both[rows:] + dot(lh, rl, dims))


def few_nn(left, right):
    return few(left, right, ((1,), (0,)))


def few_nt(left, right):
    return few(left, right, ((1,), (1,)))


def nn(left, right):
    return three(left, right, ((1,), (0,)))


def nt(left, right):
    return three(left, right, ((1,), (1,)))


def place():
    t, p = lax.axis_index("tm"), lax.axis_index("panel")
    return t // X, lax.rem(t, X), p // 2, lax.rem(p, 2), p


def call(kernel, out_shape, args, scratch=(), flops=0, name=None, space=pltpu.VMEM, light=False, grant=8):
    size = 0 if light else sum(a.size * a.dtype.itemsize for a in args)
    return pl.pallas_call(
        kernel,
        out_shape=out_shape,
        in_specs=[pl.BlockSpec(memory_space=space)] * len(args),
        out_specs=jax.tree.map(lambda _: pl.BlockSpec(memory_space=pltpu.VMEM), out_shape),
        scratch_shapes=list(scratch),
        compiler_params=pltpu.CompilerParams(vmem_limit_bytes=grant * 1024 * 1024),
        cost_estimate=pl.CostEstimate(flops=int(flops * 6 * N**3), bytes_accessed=size, transcendentals=0),
        name=name,
    )(*args)


def shape(dims, dtype=F32):
    return jax.ShapeDtypeStruct(dims, dtype)


def band_kernel(*refs):
    sources, (band, offset), places, arrived = refs[:5], refs[5:7], refs[7:12], refs[12]
    copies = [pltpu.make_async_copy(a, b, arrived.at[i]) for i, (a, b) in enumerate(zip(sources, places))]
    for copy in copies:
        copy.start()
    for copy in copies:
        copy.wait()
    cond_cov, pred_mean, correction, spread, observed = places
    _, _, _, _, p = place()
    block = lax.broadcasted_iota(jnp.int32, (2, BAND), 1) // 8
    seen = jnp.zeros((2, BAND), F32)
    for i in range(4):
        seen = seen + jnp.where(block == i, observed[:, i : i + 1].astype(F32), 0.0)
    value = pred_mean[...] + seen * correction[...]
    missing = (1.0 - seen) * spread[...]
    offset[...] = value
    lane = lax.broadcasted_iota(jnp.int32, (BAND, N), 1) - p * BAND
    diagonal = lane == lax.broadcasted_iota(jnp.int32, (BAND, N), 0)
    own = jnp.logical_and(lane[:8] >= 0, lane[:8] < BAND)
    wide = jnp.concatenate([jnp.concatenate([part] * 16, axis=1) for part in (missing, value)], axis=0)
    band[0:BAND, :] = cond_cov[0] + jnp.where(diagonal, wide[0:1, :], 0.0)
    band[BAND : 2 * BAND, :] = cond_cov[1] + jnp.where(diagonal, wide[1:2, :], 0.0)
    rows = jnp.concatenate([wide[2:4, :], jnp.zeros((6, N), F32)], axis=0)
    band[2 * BAND :, :] = jnp.where(own, rows, 0.0)


def z_pieces(pieces, rows):
    chip, r1, s1, r2, s2, r3, s3, r4, s4 = pieces
    _, _, z, core, _ = place()
    way = 2 * core - 1
    band = lambda away, c: 2 * lax.rem(z + away + Z, Z) + c
    found = [(chip, 0, band(0, core)), (chip, rows, band(0, 1 - core))]
    for i, (r, s) in enumerate(((r1, s1), (r2, s2), (r3, s3)), 1):
        found += [(r, 0, band(way * i, core)), (r, rows, band(way * i, 1 - core))]
        found += [(s, 0, band(-way * i, 1 - core)), (s, rows, band(-way * i, core))]
    return found + [(r4, 0, band(4, core)), (s4, 0, band(4, 1 - core))]


def half_pieces(pieces, at, lead, height):
    r1, s1, r2, s2 = pieces
    _, _, _, core, _ = place()
    way = 2 * core - 1
    near, far = pl.multiple_of(core * height, height), pl.multiple_of((1 - core) * height, height)
    one, two, three_ = lax.rem(at + way + 4, 4), lax.rem(at - way + 4, 4), lax.rem(at + 2, 4)
    return [
        (r1, lead, one, near),
        (r1, lead + height, one, far),
        (s1, lead, two, far),
        (s1, lead + height, two, near),
        (r2, lead, three_, near),
        (s2, lead, three_, far),
    ]


def store_rolled(dest, lead, whole, core, height):
    near, far = pl.multiple_of(core * height, height), pl.multiple_of((1 - core) * height, height)
    dest[lead : lead + height, :] = whole[pl.ds(near, height), :]
    dest[lead + height : lead + 2 * height, :] = whole[pl.ds(far, height), :]


def triangle():
    return (
        lax.broadcasted_iota(jnp.int32, (HALF, HALF), 0) - lax.broadcasted_iota(jnp.int32, (HALF, HALF), 1)
    )


def pack(dest, cov, vec, scratch, core):
    below = triangle()
    last = cov[HALF:, HALF:]
    scratch[:, :HALF] = cov[:HALF, HALF:]
    scratch[:, HALF:] = jnp.where(below >= 0, cov[:HALF, :HALF], last)
    dest[0:1, :] = vec
    dest[1:2, :HALF] = jnp.sum(jnp.where(below == 0, last, 0.0), axis=0, keepdims=True)
    dest[1:2, HALF:] = jnp.zeros((1, HALF), F32)
    dest[2:8, :] = jnp.zeros((6, N), F32)
    store_rolled(dest, 8, scratch, core, HALF // 2)


def unpack(packed, heads, at, store):
    below = triangle()
    side, mixed = packed[at, :, :HALF], packed[at, :, HALF:]
    turned = mixed.T
    store(0, 0, jnp.where(below >= 0, mixed, turned))
    store(0, HALF, side)
    store(HALF, 0, side.T)
    store(HALF, HALF, jnp.where(below < 0, mixed, jnp.where(below == 0, heads[at, 1:2, :HALF], turned)))


def compose_gain_kernel(*refs):
    pieces, (a0h, a0l, a1h, a1l, bh, bl, sent, b) = refs[:9], refs[9:]
    _, _, _, core, _ = place()
    kept = jnp.where(lax.axis_index("tm") == 15, 0.0, 1.0)
    for source, first, band in z_pieces(pieces, 2 * BAND):
        row = pl.multiple_of(band * BAND, BAND)
        a0h[pl.ds(row, BAND), :], a0l[pl.ds(row, BAND), :] = split(source[first : first + BAND, :])
        a1h[pl.ds(row, BAND), :], a1l[pl.ds(row, BAND), :] = split(
            source[first + BAND : first + 2 * BAND, :] * kept
        )
    b[...] = nn((a0h[...], a0l[...]), (a1h[...], a1l[...]))
    bh[...], bl[...] = split(b[...])
    store_rolled(sent, 0, b, core, HALF)


def congruence(left, state, add, add_vec):
    moved = nt(split(state[...]), left)
    state[:N, :] = nn(left, split(moved[:N])) + add
    state[N:, :] = moved[N:] + add_vec


def compose_cov_kernel(*refs):
    pieces, (a0h, a0l, offset), (cov_bands, offsets, sent, state, cov0, scratch) = refs[:9], refs[9:12], refs[12:]
    _, _, _, core, p = place()
    pads = jnp.zeros((8, N), F32)
    for source, first, band in z_pieces(pieces, 2 * BAND + 8):
        row = pl.multiple_of(band * BAND, BAND)
        cov0[pl.ds(row, BAND), :] = source[first : first + BAND, :]
        state[pl.ds(row, BAND), :] = source[first + BAND : first + 2 * BAND, :]
        pads = pads + source[first + 2 * BAND : first + 2 * BAND + 8, :]
    state[N:, :] = jnp.broadcast_to(pads[1:2], (16, N))
    row = pl.multiple_of(p * BAND, BAND)
    cov_bands[BAND:, :] = state[pl.ds(row, BAND), :]
    moved = nt(split(state[N:, :]), (a0h[pl.ds(row, BAND), :], a0l[pl.ds(row, BAND), :]))
    offsets[0:1, :] = moved[0:1] + offset[0:1, :]
    offsets[1:2, :] = offset[1:2, :]
    congruence((a0h[...], a0l[...]), state, cov0[...], jnp.broadcast_to(pads[0:1], (16, N)))
    cov_bands[:BAND, :] = state[pl.ds(row, BAND), :]
    pack(sent, state[:N, :], state[N : N + 1, :], scratch, core)


def row_gain_kernel(ownh, ownl, r1, s1, r2, s2, s3, bh, bl, sent, ph, plo, total):
    _, x, _, core, _ = place()
    bh[x], bl[x] = ownh[...], ownl[...]
    for source, first, at, row in half_pieces((r1, s1, r2, s2), x, 0, HALF):
        height = source.shape[0] if source is s2 else HALF
        bh[at, pl.ds(row, height), :], bl[at, pl.ds(row, height), :] = split(source[first : first + height, :])
    row = pl.multiple_of((1 - core) * HALF + HALF // 2, HALF // 2)
    at = lax.rem(x + 2, X)
    bh[at, pl.ds(row, HALF // 2), :], bl[at, pl.ds(row, HALF // 2), :] = split(s3[...])
    gain = (bh[3], bl[3])

    def keep(k, value):
        @pl.when(x == k)
        def _():
            ph[...], plo[...] = value

    keep(3, gain)
    keep(2, gain)
    gain = split(nn((bh[2], bl[2]), gain))
    keep(1, gain)
    gain = split(nn((bh[1], bl[1]), gain))
    keep(0, gain)
    total[...] = nn((bh[0], bl[0]), gain)
    store_rolled(sent, 0, total, core, HALF)


def row_cov_kernel(
    own, r1, s1, r2, s2, bh, bl, sent, suffix, suffix_vec, packed, heads, cov, state, scratch
):
    _, x, _, core, _ = place()
    near, far = (pl.multiple_of(c * HALF // 2, HALF // 2) for c in (core, 1 - core))
    own_halves = [(own, 8, x, near), (own, 8 + HALF // 2, x, far)]
    for source, first, at, row in own_halves + half_pieces((r1, s1, r2, s2), x, 8, HALF // 2):
        packed[at, pl.ds(row, HALF // 2), :] = source[first : first + HALF // 2, :]
        heads[at] = source[0:8, :]
    vecs = lambda k: jnp.broadcast_to(heads[k, 0:1, :], (16, N))

    def into(dest):
        def store(row, column, value):
            dest[row : row + HALF, column : column + HALF] = value

        return store

    unpack(packed, heads, 3, into(state))
    state[N:, :] = vecs(3)

    @pl.when(x >= 2)
    def _():
        suffix[...], suffix_vec[...] = state[:N, :], state[N : N + 8, :]

    for k in (2, 1, 0):
        unpack(packed, heads, k, into(cov))
        congruence((bh[k], bl[k]), state, cov[...], vecs(k))
        if k:

            @pl.when(x == k - 1)
            def _():
                suffix[...], suffix_vec[...] = state[:N, :], state[N : N + 8, :]

    pack(sent, state[:N, :], state[N : N + 1, :], scratch, core)


def mirrored(packed, heads, high, low):
    def store(row, column, value):
        at = (slice(row, row + HALF), slice(column, column + HALF))
        high[at], low[at] = split(value)

    unpack(packed, heads, 0, store)


def mean_of(head, left):
    return few_nt(split(jnp.broadcast_to(head, (16, N))), left)


def own_kernel(
    a1h, a1l, bh, bl, ph, plo, suffix, suffix_vec, cov_bands, vh, vl, base, mean, g1h, g1l, g0h, g0l
):
    _, x, _, _, p = place()
    row = pl.multiple_of(p * BAND, BAND)
    band = tuple(
        jnp.concatenate([one[pl.ds(row, BAND), :], zero[pl.ds(row, BAND), :]], axis=0)
        for one, zero in ((a1h, bh), (a1l, bl))
    )
    one, zero = (a1h[...], a1l[...]), (bh[...], bl[...])
    mean[...] = jnp.zeros_like(mean)
    base[:BAND, :] = cov_bands[BAND:, :]
    base[BAND:, :] = cov_bands[:BAND, :]

    @pl.when(x == X - 1)
    def _():
        g1h[...], g1l[...] = one
        g0h[...], g0l[...] = zero

    @pl.when(x < X - 1)
    def _():
        past = few_nn(band, split(suffix[...]))
        base[:BAND, :] += few_nt(split(past[:BAND]), one)
        base[BAND:, :] += few_nt(split(past[BAND:]), zero)
        mean[...] = mean_of(suffix_vec[0:1, :], band)
        g1h[...], g1l[...] = split(nn(one, (ph[...], plo[...])))
        g0h[...], g0l[...] = split(nn(zero, (ph[...], plo[...])))

    vh[...] = jnp.concatenate([g1h[pl.ds(row, BAND), :], g0h[pl.ds(row, BAND), :]], axis=0)
    vl[...] = jnp.concatenate([g1l[pl.ds(row, BAND), :], g0l[pl.ds(row, BAND), :]], axis=0)


def above_kernel(t1, ts, vh, vl, th, tl, wh, wl):
    y, _, _, core, _ = place()
    for mine, source in ((0, ts), (1, t1)):

        @pl.when(jnp.logical_and(core == mine, y < 2))
        def _():
            th[HALF:, :], tl[HALF:, :] = split(source[:HALF, :])
            th[:HALF, :], tl[:HALF, :] = split(source[HALF:, :])
            wh[...], wl[...] = split(few_nn((vh[...], vl[...]), (th[...], tl[...])))


def near_kernel(d1, ds, vh, vl, mean_in, belowh, belowl, below_vec, near, mean, packed, heads, dh, dl):
    y, _, _, core, _ = place()
    near[...] = jnp.zeros_like(near)
    mean[...] = mean_in[...]
    quarter = HALF // 2

    def take(source, first):
        packed[0, first * quarter : (first + 1) * quarter, :] = source[8 : 8 + quarter, :]
        packed[0, (1 - first) * quarter : (2 - first) * quarter, :] = source[8 + quarter :, :]
        heads[0] = source[0:8, :]

    for mine, above, below in ((0, ds, d1), (1, d1, ds)):

        @pl.when(jnp.logical_and(core == mine, y < 3))
        def _():
            take(above, 1)
            mirrored(packed, heads, dh, dl)
            near[...] = few_nn((vh[...], vl[...]), (dh[...], dl[...]))
            mean[...] += mean_of(heads[0, 0:1, :], (vh[...], vl[...]))

        @pl.when(jnp.logical_and(core == mine, y == 0))
        def _():
            take(below, 0)
            mirrored(packed, heads, belowh, belowl)
            below_vec[...] = heads[0]


def middle_kernel(t2, ts, wh, wl, belowh, belowl, below_vec, mean, beyond, mean_out, th, tl):
    y, _, _, core, _ = place()
    beyond[...] = jnp.zeros_like(beyond)
    mean_out[...] = mean[...]

    @pl.when(y == 0)
    def _():
        mine, its = (pl.multiple_of(c * HALF, HALF) for c in (core, 1 - core))
        th[pl.ds(mine, HALF), :], tl[pl.ds(mine, HALF), :] = split(t2[...])
        th[pl.ds(its, HALF), :], tl[pl.ds(its, HALF), :] = split(ts[...])
        far = (th[...], tl[...])
        left = split(few_nn((wh[...], wl[...]), far))
        mean_out[...] += mean_of(below_vec[0:1, :], left)
        beyond[...] = few_nt(split(few_nn(left, (belowh[...], belowl[...]))), far)


def last_kernel(
    d2, ds, beyond, near, base, mean_in, wh, wl, th, tl, g1h, g1l, g0h, g0l, offsets,
    mean, out, packed, heads, dh, dl, moved, row_mean,
):
    y, x, _, core, _ = place()
    moved[...] = near[...]
    row_mean[...] = mean_in[...]

    @pl.when(y < 2)
    def _():
        quarter = HALF // 2
        packed[0, pl.ds(pl.multiple_of(core * quarter, quarter), quarter), :] = d2[8:, :]
        packed[0, pl.ds(pl.multiple_of((1 - core) * quarter, quarter), quarter), :] = ds[8:, :]
        heads[0] = d2[0:8, :]
        mirrored(packed, heads, dh, dl)
        left = (wh[...], wl[...])
        row_mean[...] += mean_of(heads[0, 0:1, :], left)
        past = few_nn(left, (dh[...], dl[...])) + beyond[...]
        moved[...] += few_nt(split(past), (th[...], tl[...]))

    out[1] = few_nt(split(moved[:BAND, :]), (g1h[...], g1l[...])) + base[:BAND, :]
    out[0] = few_nt(split(moved[BAND:, :]), (g0h[...], g0l[...])) + base[BAND:, :]
    mean[1:2, :] = row_mean[0:1, :BAND] + offsets[1:2, :]
    mean[0:1, :] = row_mean[0:1, BAND : 2 * BAND] + offsets[0:1, :]


def device(y, x, z, core):
    return ((y % Y) * X + x % X) * 16 + (z % Z) * 2 + core


def perm(dy, dx, dz):
    return [
        (device(y, x, z, c), device(y + (1 - 2 * c) * dy, x + (1 - 2 * c) * dx, z + (1 - 2 * c) * dz, c))
        for y in range(Y)
        for x in range(X)
        for z in range(Z)
        for c in range(2)
    ]


AXES = ("tm", "panel")
ROUND_Y, ROUND_X, ROUND_Z, TWO_Z = perm(1, 0, 0), perm(0, 1, 0), perm(0, 0, 1), perm(0, 0, 2)
SWAP = [(i, i ^ 1) for i in range(256)]


def swap(piece):
    return lax.ppermute(piece, AXES, SWAP)


def gather_z(first, second):
    rows, now = first.rows, first.now
    r1 = hop(now, ROUND_Z)
    r2, r3 = hop(r1, ROUND_Z), hop(r1, TWO_Z)
    r4 = hop(r2[:rows], TWO_Z)
    for _ in range(4):
        second.go()
    return [now, r1, swap(r1), r2, swap(r2), r3, swap(r3), r4, swap(r4)], second.finish()


class Turn:
    def __init__(self, own):
        self.rows, self.hop, self.pieces = own.shape[0], 0, []
        self.near = swap(own)
        below, above = ((0, self.rows, 0), (0, 0, 0)), ((self.rows, 0, 0), (0, 0, 0))
        self.now = lax.pad(own, 0.0, below) + lax.pad(self.near, 0.0, above)

    def go(self):
        self.pieces += [self.now, swap(self.now)] if self.hop else [self.now]
        self.hop += 1
        self.now = hop(self.now if self.hop < 4 else self.now[: self.rows], ROUND_Z)

    def finish(self):
        return [*self.pieces, self.now, swap(self.now)]


def together(*values):
    return lax.optimization_barrier(values)


def after(value, *others):
    return together(value, *others)[0]


def hop(sent, way):
    return lax.ppermute(sent, AXES, way)


def first_half(sent):
    return sent[: (sent.shape[0] + 8) // 16 * 8]


def shards(gain, cond_cov, pred_mean, correction, spread, observed):
    square, row8, half = shape((N, N)), shape((8, N)), shape((N, N), BF16)
    first = Turn(gain.reshape(2 * BAND, N))
    args = (cond_cov, pred_mean, correction, spread[None, :], observed)
    band, offset = call(
        band_kernel,
        (shape((2 * BAND + 8, N)), shape((2, BAND))),
        args,
        (*[pltpu.VMEM(a.shape, a.dtype) for a in args[:5]], pltpu.SemaphoreType.DMA((5,))),
        name="band",
        space=pltpu.HBM,
        grant=60,
    )
    a_pieces, c_pieces = gather_z(first, Turn(band))
    a0h, a0l, a1h, a1l, b0h, b0l, sent = call(
        compose_gain_kernel,
        (half, half, half, half, half, half, square),
        a_pieces,
        (pltpu.VMEM((N, N), F32),),
        flops=1,
        name="compose_gain",
    )
    b1 = hop(sent, ROUND_X)
    state = pltpu.VMEM((N + 16, N), F32)
    scratch = pltpu.VMEM((HALF, N), F32)
    packed_four = (pltpu.VMEM((4, HALF, N), F32), pltpu.VMEM((4, 8, N), F32))
    cov_bands, offsets, c0 = call(
        compose_cov_kernel,
        (shape((2 * BAND, N)), shape((2, BAND)), shape((HALF + 8, N))),
        (*c_pieces, a0h, a0l, offset),
        (state, pltpu.VMEM((N, N), F32), scratch),
        flops=9,
        name="compose_cov",
    )
    c1 = hop(c0, ROUND_X)
    b2, c2 = hop(first_half(after(b1, offsets)), ROUND_X), hop(first_half(c1), ROUND_X)
    c_near, c_far = swap(c1), swap(c2)
    b_pieces, c_pieces = (b1, swap(b1), b2, after(swap(b2[:128]), c_near), swap(b2[128:])), (c1, c_near, c2, c_far)
    four = shape((4, N, N), BF16)
    bh, bl, sent, ph, plo = call(
        row_gain_kernel,
        (four, four, square, half, half),
        (b0h, b0l, *b_pieces),
        (pltpu.VMEM((N, N), F32),),
        name="row_gain",
        light=True,
    )
    t1 = hop(after(sent, c2), ROUND_Y)
    sent, suffix, suffix_vec = call(
        row_cov_kernel,
        (shape((HALF + 8, N)), square, row8),
        (c0, *c_pieces, bh, bl),
        (*packed_four, pltpu.VMEM((N, N), F32), state, scratch),
        flops=6,
        name="row_cov",
    )
    d1 = hop(sent, ROUND_Y)
    rows, vecs = shape((2 * BAND, N), BF16), shape((16, 2 * BAND))
    plain = shape((2 * BAND, N))
    one_packed = (pltpu.VMEM((1, HALF, N), F32), pltpu.VMEM((1, 8, N), F32))
    whole = (pltpu.VMEM((N, N), BF16), pltpu.VMEM((N, N), BF16))
    vh, vl, base, mean, *taken = call(
        own_kernel,
        (rows, rows, plain, vecs, half, half, half, half),
        (a1h, a1l, b0h, b0l, ph, plo, suffix, suffix_vec, cov_bands),
        flops=1,
        name="own",
    )
    t2 = hop(first_half(after(t1, mean)), ROUND_Y)
    t_near, d_near = swap(after(t1, base)), swap(d1)
    th, tl, wh, wl = call(
        above_kernel, (half, half, rows, rows), (t1, t_near, vh, vl), flops=1, name="above"
    )
    d2 = hop(first_half(d1), ROUND_Y)
    belowh, belowl, below_vec, near, mean = call(
        near_kernel,
        (half, half, row8, plain, vecs),
        (d1, d_near, vh, vl, mean),
        (*one_packed, *whole),
        flops=1,
        name="near",
    )
    t_far, d_far = swap(after(t2, d2)), swap(d2)
    beyond, mean = call(
        middle_kernel,
        (plain, vecs),
        (t2, t_far, wh, wl, belowh, belowl, below_vec, mean),
        whole,
        flops=2,
        name="middle",
    )
    return call(
        last_kernel,
        (shape((2, BAND)), shape((2, BAND, N))),
        (d2, d_far, beyond, near, base, mean, wh, wl, th, tl, *taken, offsets),
        (*one_packed, *whole, pltpu.VMEM((2 * BAND, N), F32), pltpu.VMEM((16, 2 * BAND), F32)),
        flops=1,
        name="last",
    )


def solution(mesh):
    placed = (
        P("tm", "panel", None),
        P("tm", "panel", None),
        P("tm", "panel"),
        P("tm", "panel"),
        P("panel"),
        P("tm", "panel"),
    )
    return jax.shard_map(
        shards,
        mesh=mesh,
        in_specs=placed,
        out_specs=(P("tm", "panel"), P("tm", "panel", None)),
        check_vma=False,
    )
```
